512 devices in a mesh: replica: 16 (over y, core), shard: 32 (over z, x).
Axes of the slice: x: 4, y: 8, z: 8, core: 2. Of those that a mesh axis runs over, the one named last changes fastest.
Arguments:
- item_table: float32 [65536, 128], P('shard')
- neighbours: int32 [16384, 128], P(('replica', 'shard')), may hold values from 0 to 65535, as said below
- confidence: float32 [16384, 128], P(('replica', 'shard')), may hold values from 0.1 to 10
- valid_counts: int32 [16384], P(('replica', 'shard')), may hold values from 1 to 128, as said below
- row_targets: int32 [16384], P('shard'), may hold values from 0 to 511, as said below
Outputs:
- user_factors: float32 [16384, 128], P('shard')
The draws below stay inside these ranges and needn't reach their ends.
Inputs may be any that keep to these rules, and one draw needn't show every extreme that they name: `neighbours`: in each aligned block of 32 rows, at most 192 entries lie in any one aligned range of 2048 ids, and this most is reached in every block. `valid_counts`: some row reaches the most. `row_targets`: each aligned block of 512 entries holds every number of its range once.
All inputs are finite; a program needn't handle non-finite values.
Results may differ from the reference program's by a relative error of at most 0.0007.
Values sent between devices are 32-bit elements; how exact they have to be, the bound alone decides.
A program may use at most 64 MiB of HBM per device.

```python
import math
import jax
import jax.numpy as jnp
from jax import lax

D = 128
K = 128
B_DEV = 32
TAB_DEV = 2048
ITERS = 4
GROUPS = 16
USERS = 16384
ITEMS = 65536


def draw_item_table(key, part):
    key = jax.random.fold_in(key, 11)
    k_row, k_col, k_base = jax.random.split(key, 3)
    pos = jnp.arange(ITEMS, dtype=jnp.float32) / jnp.float32(max(ITEMS - 1, 1))
    rise = 0.6 * jnp.power(3.0, pos)
    row = rise * jnp.power(10.0, jax.random.uniform(k_row, (ITEMS,), jnp.float32) - 0.5)
    col = jnp.power(10.0, jax.random.uniform(k_col, (1, D), jnp.float32) * 0.6 - 0.3)
    base = jax.random.normal(k_base, (ITEMS, D), jnp.float32)
    return (base * row[:, None] * col).astype(jnp.float32)


def draw_neighbours(key, part):
    key = jax.random.fold_in(key, 12)
    k_hot, k_perm, k_local = jax.random.split(key, 3)
    nshard = ITEMS // TAB_DEV
    slots = B_DEV * K
    cap = slots // nshard + slots // (2 * nshard)
    blocks = USERS // B_DEV
    hot = jax.random.randint(k_hot, (), 0, nshard)
    perms = jax.vmap(lambda k: jax.random.permutation(k, slots))(jax.random.split(k_perm, blocks))
    rest = perms - cap
    other = jnp.mod(jnp.maximum(rest, 0), nshard - 1)
    other = other + (other >= hot).astype(jnp.int32)
    owner = jnp.where(perms < cap, hot, other).astype(jnp.int32)
    local = jax.random.randint(k_local, (blocks, slots), 0, TAB_DEV)
    return (owner * TAB_DEV + local).reshape(USERS, K).astype(jnp.int32)


def draw_valid_counts(key, part):
    key = jax.random.fold_in(key, 13)
    k_a, k_b, k_r = jax.random.split(key, 3)
    first = jax.random.randint(k_a, (USERS,), 1, K + 1)
    second = jax.random.randint(k_b, (USERS,), 1, K + 1)
    picked = jax.random.randint(k_r, (), 0, USERS)
    counts = jnp.maximum(first, second)
    return jnp.where(jnp.arange(USERS) == picked, K, counts).astype(jnp.int32)


def draw_row_targets(key, part):
    key = jax.random.fold_in(key, 14)
    per = GROUPS * B_DEV
    nshard = USERS // per
    perms = jax.vmap(lambda k: jax.random.permutation(k, per))(jax.random.split(key, nshard))
    return perms.reshape(USERS).astype(jnp.int32)


def steps_of(key, shape, cuts, low, largest):
    loudness = 1.0
    for position, blocks in cuts:
        steps = jax.random.uniform(jax.random.fold_in(jax.random.fold_in(key, 6), position), (blocks,), jnp.float32, low / len(cuts), largest / len(cuts))
        loudness = loudness * jnp.repeat(jnp.exp(steps), shape[position] // blocks).reshape((-1,) + (1,) * (len(shape) - 1 - position))
    return loudness


def setup_inputs(seed: int = 0) -> dict:
    keys = jax.random.split(jax.random.key(seed), 6)
    return {
        "item_table": draw_item_table(jax.random.fold_in(keys[5], 71), 0),
        "neighbours": draw_neighbours(jax.random.fold_in(keys[5], 71), 0),
        "confidence": jnp.clip(jnp.exp(math.log(10.0) - 4.6051702 * jax.random.uniform(keys[2], (USERS, K), jnp.float32) ** steps_of(keys[2], (USERS, K), ((0, 512),), -0.2, 0.2)), 0.1, 10.0),
        "valid_counts": draw_valid_counts(jax.random.fold_in(keys[5], 71), 0),
        "row_targets": draw_row_targets(jax.random.fold_in(keys[5], 71), 0),
    }


HI = lax.Precision.HIGHEST

def solve_block(rows, weights, counts, scaled):
    width = rows.shape[2]
    used = jnp.arange(rows.shape[1])[None, :] < counts[:, None]
    wmask = jnp.where(used, weights, 0.0)
    bmask = jnp.where(used, 1.0 + weights, 0.0)
    rhs = jnp.einsum('uk,ukd->ud', bmask, rows, precision=HI) / jnp.sqrt(jnp.float32(width))

    def apply_op(vec):
        proj = jnp.einsum('ukd,ud->uk', rows, vec, precision=HI)
        coef = wmask * proj / width
        return 1.0 * vec + jnp.dot(vec, scaled, precision=HI) + jnp.einsum('uk,ukd->ud', coef, rows, precision=HI)
    sol = jnp.zeros_like(rhs)
    resid = rhs
    direc = rhs
    rr_now = lax.optimization_barrier(jnp.sum(resid * resid, axis=1, keepdims=True))
    for step in range(ITERS):
        image = apply_op(direc)
        alpha = rr_now / lax.optimization_barrier(jnp.sum(direc * image, axis=1, keepdims=True))
        sol = sol + alpha * direc
        resid = resid - alpha * image
        rr_next = lax.optimization_barrier(jnp.sum(resid * resid, axis=1, keepdims=True))
        direc = resid + rr_next / rr_now * direc
        rr_now = rr_next
    return sol

def reference(item_table, neighbours, confidence, valid_counts, row_targets):
    gram = jnp.dot(item_table.T, item_table, precision=HI)
    scaled = 2.0 / ITEMS * gram
    blocks = USERS // B_DEV
    nb = neighbours.reshape(blocks, B_DEV, K)
    cf = confidence.reshape(blocks, B_DEV, K)
    ct = valid_counts.reshape(blocks, B_DEV)

    def one(args):
        ids, conf, cnt = args
        return solve_block(item_table[ids], conf, cnt, scaled)
    solved = lax.map(one, (nb, cf, ct))
    nshard = ITEMS // TAB_DEV
    per = GROUPS * B_DEV
    arranged = solved.reshape(GROUPS, nshard, B_DEV, D).transpose(1, 0, 2, 3).reshape(nshard, per, D)
    targets = row_targets.reshape(nshard, per)

    def place(vals, idx):
        return jnp.zeros((per, D), jnp.float32).at[idx].set(vals)
    return jax.vmap(place)(arranged, targets).reshape(USERS, D)
```

```python
import functools
import math

import jax
import jax.numpy as jnp
from jax import lax
from jax.experimental import pallas as pl
from jax.experimental.pallas import tpu as pltpu
from jax.sharding import PartitionSpec as P

ITERS = 4
NX, NZ, NY = 4, 8, 8
D = 128
K = 128
U = 32
TAB = 2048
ITEMS = 65536
CAP = 192
SLOTS = NX * CAP
KH = SLOTS // 128
MESH = pl.DeviceIdType.MESH
F32, BF16, I32 = jnp.float32, jnp.bfloat16, jnp.int32
ORDER = (1, 7, 2, 6, 3, 5, 4)
NT = (((1,), (1,)), ((), ()))
TN = (((0,), (0,)), ((), ()))


def split2(v):
    hi = v.astype(BF16)
    lo = (v - hi.astype(F32)).astype(BF16)
    return hi, lo


def split3(v):
    hi = v.astype(BF16)
    rest = v - hi.astype(F32)
    mid = rest.astype(BF16)
    lo = (rest - mid.astype(F32)).astype(BF16)
    return hi, mid, lo


def iota(shape, dim):
    return lax.broadcasted_iota(I32, shape, dim)


def kernel(
    counts, ids_ref, conf_ref, targ_ref, table,
    out_ref,
    tab0, tab1, tab2, tab3, code_s, kl_s, val_s, a_s, b_s, ent_send, ent, idv, ids_smem, found, fmat, mw, gacc,
    psend, pbuf, qsend, qbuf, gat, place,
    own_sem, tx_sem, trx_sem, tfwd_sem, ts_sem, tsr_sem, es_sem, er_sem, id_sem, ps_sem, pr_sem, qs_sem, qr_sem,
    ys_sem, yr_sem, ss_sem, sr_sem,
):
    r = lax.axis_index("replica")
    s = lax.axis_index("shard")
    z, x = lax.div(s, NX), lax.rem(s, NX)
    y, core = lax.div(r, 2), lax.rem(r, 2)

    def zpeer(dz):
        return (r, lax.rem(z + dz, NZ) * NX + x)

    def xpeer(dx):
        return (r, z * NX + lax.rem(x + dx, NX))

    def ypeer(dy):
        return (lax.rem(y + dy, NY) * 2 + core, s)

    sibling = (y * 2 + 1 - core, s)

    own = pltpu.make_async_copy(table, tab0, own_sem)
    own.start()

    barrier = pltpu.get_barrier_semaphore()
    peers = [xpeer(1), xpeer(3), sibling]
    peers += [zpeer(dz) for dz in range(1, NZ)] + [ypeer(dy) for dy in range(1, NY)]
    for peer in peers:
        pl.semaphore_signal(barrier, inc=1, device_id=peer, device_id_type=MESH)
    pl.semaphore_wait(barrier, len(peers))

    half = TAB // 2
    piece = half // 2

    def rows_of(c):
        return pl.ds(pl.multiple_of(core * half + c * piece, piece), piece)

    def remote(src, dst, send, recv, peer):
        return pltpu.make_async_remote_copy(
            src_ref=src, dst_ref=dst, send_sem=send, recv_sem=recv, device_id=peer, device_id_type=MESH)

    right = [remote(table.at[rows_of(c)], tab3.at[rows_of(c)], tx_sem.at[c], trx_sem.at[c], xpeer(1)) for c in range(2)]
    left = [remote(table.at[rows_of(c)], tab1.at[rows_of(c)], tx_sem.at[2 + c], trx_sem.at[2 + c], xpeer(3)) for c in range(2)]
    fwd_right = remote(tab3.at[rows_of(0)], tab2.at[rows_of(0)], tfwd_sem.at[0], trx_sem.at[4], xpeer(1))
    fwd_left = remote(tab1.at[rows_of(1)], tab2.at[rows_of(1)], tfwd_sem.at[1], trx_sem.at[5], xpeer(3))
    arrivals = [(tab3, 0), (tab1, 1), (tab3, 1), (tab1, 0), (tab2, 0), (tab2, 1)]
    to_sib = [
        remote(t.at[rows_of(c)], t.at[rows_of(c)], ts_sem.at[i], tsr_sem.at[i], sibling)
        for i, (t, c) in enumerate(arrivals)
    ]
    right[0].start()
    left[1].start()
    right[1].start()
    left[0].start()

    ids = ids_ref[...]
    owner = lax.shift_right_logical(ids, 11)
    local = ids & (TAB - 1)
    rowi = iota((U, K), 0)
    lane = iota((U, K), 1)
    cnt = jnp.zeros((U, K), I32)
    for u in range(U):
        cnt = jnp.where(rowi == u, counts[u], cnt)
    used = lane < cnt
    key = jnp.where(used, owner, -1)
    e_all = jnp.concatenate(
        [jnp.where(key == o, 1.0, 0.0).astype(BF16) for o in range(NX * NZ)], axis=0)
    br, bc = iota((256, 256), 0), iota((256, 256), 1)
    lower = jnp.where((lax.shift_right_logical(br, 5) == lax.shift_right_logical(bc, 5)) & (bc < br), 1.0, 0.0).astype(BF16)
    x_all = jnp.concatenate(
        [jnp.dot(lower, e_all[i * 256:(i + 1) * 256], preferred_element_type=F32).astype(BF16) for i in range(4)], axis=0)
    tr, tc = iota((256, 128), 0), iota((256, 128), 1)
    tri = jnp.where((tr >= 128) | (tr < tc), 1.0, 0.0).astype(BF16)
    pos_all = jnp.dot(jnp.concatenate([e_all, x_all], axis=1), tri, preferred_element_type=F32)
    pos = jnp.zeros((U, K), F32)
    for o in range(NX * NZ):
        pos = jnp.where(key == o, pos_all[o * U:(o + 1) * U], pos)
    slot = (owner & (NX - 1)) * CAP + pos.astype(I32)
    code_s[...] = jnp.where(used, lax.shift_right_logical(owner, 2) * 8 + lax.shift_right_logical(slot, 7), -1)
    kl_s[...] = slot & 127
    conf = conf_ref[...]
    m1, m2, m3 = split3(conf)
    val_s[0] = (local & 0x700).astype(F32)
    val_s[1] = (local & 0xFF).astype(F32)
    val_s[2] = (rowi + 1).astype(F32)
    val_s[3] = m1.astype(F32)
    val_s[4] = m2.astype(F32)
    val_s[5] = m3.astype(F32)
    sub = iota((128, 128), 0)

    def build(u, carry):
        cols = pl.ds(pl.multiple_of(u * 128, 128), 128)
        a_s[:, cols] = jnp.where(sub == code_s[pl.ds(u, 1), :], 1.0, 0.0).astype(BF16)
        hot = sub == kl_s[pl.ds(u, 1), :]
        for c in range(6):
            b_s[c * 128:(c + 1) * 128, cols] = jnp.where(hot, val_s[c, pl.ds(u, 1), :], 0.0).astype(BF16)
        return carry

    lax.fori_loop(0, U, build, 0)
    packed = lax.dot_general(b_s[...], a_s[...], NT, preferred_element_type=F32)
    e_id = (packed[0:128] + packed[128:256]).T[0:64]
    e_user = packed[256:384].T[0:64]
    e_conf = (packed[384:512] + packed[512:640] + packed[640:768]).T[0:64]
    ent_send[:, 0:8, :] = e_id.reshape(NZ, 8, 128)
    ent_send[:, 8:16, :] = e_user.reshape(NZ, 8, 128)
    ent_send[:, 16:24, :] = e_conf.reshape(NZ, 8, 128)
    ent[z] = ent_send[z]
    ent_copies = []
    for i, dz in enumerate(ORDER):
        copy = remote(ent_send.at[lax.rem(z + dz, NZ)], ent.at[z], es_sem.at[i], er_sem.at[i], zpeer(dz))
        copy.start()
        ent_copies.append(copy)

    place[...] = jnp.where(iota((512, 512), 0) == targ_ref[...], 1.0, 0.0).astype(BF16)

    gacc[...] = jnp.zeros_like(gacc)

    def gram_of(tab):
        def step(i, carry):
            v = tab[pl.ds(pl.multiple_of(i * 512, 512), 512), :]
            hl = jnp.concatenate(split2(v), axis=1)
            gacc[...] += lax.dot_general(hl, hl, TN, preferred_element_type=F32)
            return carry
        lax.fori_loop(0, TAB // 512, step, 0)

    own.wait()
    gram_of(tab0)

    right[0].wait_recv()
    fwd_right.start()
    to_sib[0].start()
    left[1].wait_recv()
    fwd_left.start()
    to_sib[1].start()

    for copy in ent_copies:
        copy.wait_recv()
    idv[...] = ent[:, 0:8, :].astype(I32).reshape(NZ * 8, 128) & (TAB - 1)
    idcopy = pltpu.make_async_copy(idv, ids_smem, id_sem)
    idcopy.start()
    ucode = (iota((U, 128), 0) + 1).astype(F32)

    def weights(i, carry):
        for kh in range(KH):
            eq = ent[i, pl.ds(8 + kh, 1), :] == ucode
            m = ent[i, pl.ds(16 + kh, 1), :]
            mw[i, :, kh * 128:(kh + 1) * 128] = jnp.where(eq, m * (1.0 / D), 0.0)
        return carry

    lax.fori_loop(0, NZ, weights, 0)
    idcopy.wait()

    def gather(tab, rel):
        first = lax.rem(x + rel, NX) * CAP

        def step(i, carry):
            src, t = lax.div(i, 3), lax.rem(i, 3)
            k0 = first + t * 64
            row = src * 8 + lax.div(k0, 128)
            col = lax.rem(k0, 128)
            base = src * SLOTS + k0
            for l in range(64):
                found[pl.ds(base + l, 1), :] = tab[pl.ds(ids_smem[row, col + l], 1), :]
            return carry

        lax.fori_loop(0, NZ * 3, step, 0)

    gather(tab0, 0)
    right[1].wait_recv()
    to_sib[2].start()
    left[0].wait_recv()
    to_sib[3].start()
    for i in (0, 2):
        to_sib[i].wait_recv()
    gather(tab3, 3)
    gram_of(tab3)
    for i in (1, 3):
        to_sib[i].wait_recv()
    gather(tab1, 1)
    gram_of(tab1)
    fwd_right.wait_recv()
    to_sib[4].start()
    fwd_left.wait_recv()
    to_sib[5].start()
    for i in (4, 5):
        to_sib[i].wait_recv()
    gather(tab2, 2)
    gram_of(tab2)

    scale = 2.0 / ITEMS
    g = (gacc[0:128, 0:128] + gacc[0:128, 128:256] + gacc[128:256, 0:128] + gacc[128:256, 128:256]) * scale
    ghl = jnp.concatenate(split2(g), axis=1)

    def convert(i, carry):
        for c in range(KH):
            v = found[pl.ds(pl.multiple_of(i * SLOTS + c * 128, 128), 128), :]
            fmat[i, c * 128:(c + 1) * 128, :] = jnp.concatenate(split2(v), axis=1)
        fmat[i, SLOTS:SLOTS + 128, :] = ghl
        return carry

    lax.fori_loop(0, NZ, convert, 0)

    def fold(res):
        return res[0:U, 0:128] + res[0:U, 128:256] + res[U:2 * U, 0:128]

    def rhs_share(i):
        parts = []
        for kh in range(KH):
            eq = ent[i, pl.ds(8 + kh, 1), :] == ucode
            m = ent[i, pl.ds(16 + kh, 1), :]
            parts.append(jnp.where(eq, (1.0 + m) * (1.0 / math.sqrt(D)), 0.0))
        hi, lo = split2(jnp.concatenate(parts, axis=1))
        return fold(jnp.dot(jnp.concatenate([hi, lo], axis=0), fmat[i, 0:SLOTS, :], preferred_element_type=F32))

    def project(i, hi, lo):
        lhs = jnp.concatenate(
            [jnp.concatenate([hi, hi], axis=1), jnp.concatenate([lo, jnp.zeros_like(lo)], axis=1)], axis=0)
        res = lax.dot_general(lhs, fmat[i, 0:SLOTS, :], NT, preferred_element_type=F32)
        return res[0:U] + res[U:2 * U]

    def share(i, p):
        hi, lo = split2(p)
        yhi, ylo = split2(mw[i] * project(i, hi, lo))
        lhs = jnp.concatenate(
            [jnp.concatenate([yhi, hi], axis=1), jnp.concatenate([ylo, lo], axis=1)], axis=0)
        return fold(jnp.dot(lhs, fmat[i], preferred_element_type=F32))

    def last_share(i, p):
        hi, lo = split2(p)
        proj = project(i, hi, lo)
        sq = mw[i] * proj * proj
        t = fold(jnp.dot(jnp.concatenate([hi, lo], axis=0), fmat[i, SLOTS:SLOTS + 128, :], preferred_element_type=F32)) * p
        for kh in range(KH):
            t = t + sq[:, kh * 128:(kh + 1) * 128]
        return t

    p_copies = [remote(psend, pbuf.at[z], ps_sem.at[i], pr_sem.at[i], zpeer(dz)) for i, dz in enumerate(ORDER)]

    def q_copy(i, dz):
        return remote(qsend.at[i], qbuf.at[NZ - dz], qs_sem.at[dz], qr_sem.at[NZ - dz], zpeer(dz))

    q_copies = [q_copy(i, dz) for i, dz in enumerate(ORDER)]

    def exchange(fn, p):
        if p is not None:
            psend[...] = p
            for copy in reversed(p_copies):
                copy.start()
        total = fn(z, p)
        for i, dz in enumerate(ORDER):
            src = lax.rem(z + dz, NZ)
            if p is not None:
                p_copies[ORDER.index(NZ - dz)].wait_recv()
                theirs = pbuf[src]
            else:
                theirs = None
            qsend[i] = fn(src, theirs)
            q_copies[i].start()
        for i in range(len(ORDER)):
            q_copies[i].wait_recv()
        for dz in range(1, NZ):
            total = total + qbuf[dz]
        for copy in q_copies:
            copy.wait_send()
        if p is not None:
            for copy in p_copies:
                copy.wait_send()
        return total

    rhs = exchange(lambda i, p: rhs_share(i), None)

    def norm(v):
        return jnp.sum(v * v, axis=1, keepdims=True)

    def iterate(_, carry):
        sol, res, p, rr = carry
        q = p + exchange(share, p)
        alpha = rr / jnp.sum(p * q, axis=1, keepdims=True)
        sol = sol + alpha * p
        res = res - alpha * q
        new = norm(res)
        return sol, res, res + (new / rr) * p, new

    carry = (jnp.zeros_like(rhs), rhs, rhs, norm(rhs))
    sol, res, p, rr = lax.fori_loop(0, ITERS - 1, iterate, carry)
    pq = jnp.sum(p * p + exchange(last_share, p), axis=1, keepdims=True)
    sol = sol + (rr / pq) * p

    def group_rows(dy, c):
        return pl.ds(pl.multiple_of((lax.rem(y + dy, NY) * 2 + c) * U, U), U)

    gat[group_rows(0, core), :] = sol
    mine = gat.at[group_rows(0, core)]
    y_copies = [remote(mine, mine, ys_sem.at[dy], yr_sem.at[dy], ypeer(dy)) for dy in range(1, NY)]
    s_copies = [
        remote(gat.at[group_rows(dy, core)], gat.at[group_rows(dy, core)], ss_sem.at[dy], sr_sem.at[dy], sibling)
        for dy in range(NY)
    ]
    for copy in reversed(y_copies):
        copy.start()
    s_copies[0].start()
    for dy in (1, 7, 2, 6, 3, 5, 4):
        y_copies[NY - dy - 1].wait_recv()
        s_copies[dy].start()
    for copy in s_copies:
        copy.wait_recv()
    hml = jnp.concatenate(split3(gat[...]), axis=1)
    placed = jnp.dot(place[...], hml, preferred_element_type=F32)
    out_ref[...] = placed[:, 0:128] + placed[:, 128:256] + placed[:, 256:384]

    for copy in right + left + [fwd_right, fwd_left] + to_sib + ent_copies + y_copies + s_copies:
        copy.wait_send()


def per_device(item_table, neighbours, confidence, valid_counts, row_targets):
    vmem = pl.BlockSpec(memory_space=pltpu.VMEM)
    dma = pltpu.SemaphoreType.DMA
    return pl.pallas_call(
        kernel,
        out_shape=jax.ShapeDtypeStruct((512, D), F32),
        in_specs=[pl.BlockSpec(memory_space=pltpu.SMEM), vmem, vmem, vmem, pl.BlockSpec(memory_space=pl.ANY)],
        out_specs=vmem,
        scratch_shapes=[
            pltpu.VMEM((TAB, D), F32), pltpu.VMEM((TAB, D), F32), pltpu.VMEM((TAB, D), F32), pltpu.VMEM((TAB, D), F32),
            pltpu.VMEM((U, K), I32), pltpu.VMEM((U, K), I32), pltpu.VMEM((6, U, K), F32),
            pltpu.VMEM((128, U * K), BF16), pltpu.VMEM((6 * 128, U * K), BF16),
            pltpu.VMEM((NZ, 24, 128), F32), pltpu.VMEM((NZ, 24, 128), F32),
            pltpu.VMEM((NZ * 8, 128), I32), pltpu.SMEM((NZ * 8, 128), I32),
            pltpu.VMEM((NZ * SLOTS, D), F32), pltpu.VMEM((NZ, SLOTS + 128, 2 * D), BF16),
            pltpu.VMEM((NZ, U, SLOTS), F32), pltpu.VMEM((2 * D, 2 * D), F32),
            pltpu.VMEM((U, D), F32), pltpu.VMEM((NZ, U, D), F32),
            pltpu.VMEM((NZ - 1, U, D), F32), pltpu.VMEM((NZ, U, D), F32),
            pltpu.VMEM((512, D), F32), pltpu.VMEM((512, 512), BF16),
            dma, dma((4,)), dma((6,)), dma((2,)), dma((6,)), dma((6,)), dma((7,)), dma((7,)), dma,
            dma((7,)), dma((7,)), dma((NZ,)), dma((NZ,)), dma((NY,)), dma((NY,)), dma((NY,)), dma((NY,)),
        ],
        compiler_params=pltpu.CompilerParams(
            collective_id=0, has_side_effects=True, vmem_limit_bytes=48 * 1024 * 1024),
    )(valid_counts, neighbours, confidence, row_targets.reshape(1, 512), item_table)


def solution(mesh):
    return jax.shard_map(
        per_device,
        mesh=mesh,
        in_specs=(
            P("shard", None),
            P(("replica", "shard"), None),
            P(("replica", "shard"), None),
            P(("replica", "shard")),
            P("shard"),
        ),
        out_specs=P("shard", None),
        check_vma=False,
    )
```

```python
import math

import jax
import jax.numpy as jnp
from jax import lax
from jax.experimental import pallas as pl
from jax.experimental.pallas import tpu as pltpu
from jax.sharding import PartitionSpec as P

ITERS = 4
NX, NZ, NY = 4, 8, 8
D = 128
K = 128
U = 32
TAB = 2048
ITEMS = 65536
CAP = 192
SLOTS = NX * CAP
KH = SLOTS // 128
MESH = pl.DeviceIdType.MESH
F32, BF16, I32 = jnp.float32, jnp.bfloat16, jnp.int32
ORDER = (1, 7, 2, 6, 3, 5, 4)
FAR = (4, 3, 5, 2, 6, 1, 7)
GROUPS = ((1, 7), (2, 6), (3, 5), (4,))
NT = (((1,), (1,)), ((), ()))
TN = (((0,), (0,)), ((), ()))


def split2(v):
    hi = v.astype(BF16)
    lo = (v - hi.astype(F32)).astype(BF16)
    return hi, lo


def split3(v):
    hi = v.astype(BF16)
    rest = v - hi.astype(F32)
    mid = rest.astype(BF16)
    lo = (rest - mid.astype(F32)).astype(BF16)
    return hi, mid, lo


def iota(shape, dim):
    return lax.broadcasted_iota(I32, shape, dim)


def kernel(
    counts_hbm, ids_hbm, conf_hbm, targ_hbm, table,
    out_ref,
    counts, ids_ref, conf_ref, targ_ref,
    tab0, tab1, tab2, tab3, code_s, kl_s, val_s, a_s, b_s, ent_send, ent, ent2, idr, tt, halves, ft, mw, mb, gacc,
    psend, pbuf, qsend, qbuf, gat, place,
    in_sem, own_sem, tx_sem, trx_sem, tfwd_sem, ts_sem, tsr_sem, es_sem, er_sem, ps_sem, pr_sem, qs_sem, qr_sem,
    ys_sem, yr_sem, ss_sem, sr_sem,
):
    r = lax.axis_index("replica")
    s = lax.axis_index("shard")
    z, x = lax.div(s, NX), lax.rem(s, NX)
    y, core = lax.div(r, 2), lax.rem(r, 2)

    def zpeer(dz):
        return (r, lax.rem(z + dz, NZ) * NX + x)

    def xpeer(dx):
        return (r, z * NX + lax.rem(x + dx, NX))

    def ypeer(dy):
        return (lax.rem(y + dy, NY) * 2 + core, s)

    sibling = (y * 2 + 1 - core, s)

    barrier = pltpu.get_barrier_semaphore()
    peers = [zpeer(dz) for dz in range(1, NZ)] + [xpeer(1), xpeer(3), sibling]
    peers += [ypeer(dy) for dy in range(1, NY)]
    for peer in peers:
        pl.semaphore_signal(barrier, inc=1, device_id=peer, device_id_type=MESH)

    loads = [
        pltpu.make_async_copy(src, dst, in_sem.at[i])
        for i, (src, dst) in enumerate(
            [(ids_hbm, ids_ref), (counts_hbm, counts), (conf_hbm, conf_ref), (targ_hbm, targ_ref)])
    ]
    own = pltpu.make_async_copy(table, tab0, own_sem)
    for load in loads:
        load.start()
    own.start()

    half = TAB // 2
    piece = half // 2

    def rows_of(c):
        return pl.ds(pl.multiple_of(core * half + c * piece, piece), piece)

    def remote(src, dst, send, recv, peer):
        return pltpu.make_async_remote_copy(
            src_ref=src, dst_ref=dst, send_sem=send, recv_sem=recv, device_id=peer, device_id_type=MESH)

    right = [remote(table.at[rows_of(c)], tab3.at[rows_of(c)], tx_sem.at[c], trx_sem.at[c], xpeer(1)) for c in range(2)]
    left = [remote(table.at[rows_of(c)], tab1.at[rows_of(c)], tx_sem.at[2 + c], trx_sem.at[2 + c], xpeer(3)) for c in range(2)]
    fwd_right = remote(tab3.at[rows_of(0)], tab2.at[rows_of(0)], tfwd_sem.at[0], trx_sem.at[4], xpeer(1))
    fwd_left = remote(tab1.at[rows_of(1)], tab2.at[rows_of(1)], tfwd_sem.at[1], trx_sem.at[5], xpeer(3))
    arrivals = [(tab3, 0), (tab1, 1), (tab3, 1), (tab1, 0), (tab2, 0), (tab2, 1)]
    to_sib = [
        remote(t.at[rows_of(c)], t.at[rows_of(c)], ts_sem.at[i], tsr_sem.at[i], sibling)
        for i, (t, c) in enumerate(arrivals)
    ]

    for load in loads[:3]:
        load.wait()
    ids = ids_ref[...]
    owner = lax.shift_right_logical(ids, 11)
    local = ids & (TAB - 1)
    rowi = iota((U, K), 0)
    lane = iota((U, K), 1)
    cnt = jnp.zeros((U, K), I32)
    for u in range(U):
        cnt = jnp.where(rowi == u, counts[u], cnt)
    used = lane < cnt
    key = jnp.where(used, owner, -1)
    e_all = jnp.concatenate(
        [jnp.where(key == o, 1.0, 0.0).astype(BF16) for o in range(NX * NZ)], axis=0)
    br, bc = iota((256, 256), 0), iota((256, 256), 1)
    lower = jnp.where((lax.shift_right_logical(br, 5) == lax.shift_right_logical(bc, 5)) & (bc < br), 1.0, 0.0).astype(BF16)
    x_all = jnp.concatenate(
        [jnp.dot(lower, e_all[i * 256:(i + 1) * 256], preferred_element_type=F32).astype(BF16) for i in range(4)], axis=0)
    tr, tc = iota((256, 128), 0), iota((256, 128), 1)
    tri = jnp.where((tr >= 128) | (tr < tc), 1.0, 0.0).astype(BF16)
    pos_all = jnp.dot(jnp.concatenate([e_all, x_all], axis=1), tri, preferred_element_type=F32)
    pos = jnp.zeros((U, K), F32)
    for o in range(NX * NZ):
        pos = jnp.where(key == o, pos_all[o * U:(o + 1) * U], pos)
    pos = pos.astype(I32)
    ox = owner & (NX - 1)
    full = pos < 128
    part = jnp.where(full, lax.shift_right_logical(pos, 6), ox & 1)
    row = jnp.where(full, ox, NX + lax.shift_right_logical(ox, 1))
    code_s[...] = jnp.where(used, part * 64 + lax.shift_right_logical(owner, 2) * 8 + row, -1)
    kl_s[...] = pos & 63
    m1, m2, m3 = split3(conf_ref[...])
    val_s[0] = (local & 0x700).astype(F32)
    val_s[1] = (local & 0xFF).astype(F32)
    val_s[2] = (rowi + 1).astype(F32)
    val_s[3] = m1.astype(F32)
    val_s[4] = m2.astype(F32)
    val_s[5] = m3.astype(F32)
    sub = iota((128, 128), 0)

    def build(u, carry):
        cols = pl.ds(pl.multiple_of(u * 128, 128), 128)
        a_s[:, cols] = jnp.where(sub == code_s[pl.ds(u, 1), :], 1.0, 0.0).astype(BF16)
        hot = sub[0:64] == kl_s[pl.ds(u, 1), :]
        for c in range(6):
            b_s[c * 64:(c + 1) * 64, cols] = jnp.where(hot, val_s[c, pl.ds(u, 1), :], 0.0).astype(BF16)
        return carry

    lax.fori_loop(0, U, build, 0)
    packed = lax.dot_general(b_s[...], a_s[...], NT, preferred_element_type=F32)

    def tiles(v):
        return jnp.concatenate([v[:, 0:64], v[:, 64:128]], axis=0).T.reshape(NZ, 8, 128)

    ent_send[:, 0:8, :] = tiles(packed[0:64] + packed[64:128])
    ent_send[:, 8:16, :] = tiles(packed[128:192])
    ent_send[:, 16:24, :] = tiles(packed[192:256] + packed[256:320] + packed[320:384])
    ent[z] = ent_send[z]

    pl.semaphore_wait(barrier, len(peers))
    ent_copies = [
        remote(ent_send.at[lax.rem(z + dz, NZ)], ent.at[z], es_sem.at[i], er_sem.at[i], zpeer(dz))
        for i, dz in enumerate(ORDER)
    ]
    for copy in reversed(ent_copies):
        copy.start()
    right[0].start()
    left[1].start()
    right[1].start()
    left[0].start()

    loads[3].wait()
    place[...] = jnp.where(iota((512, 512), 0) == targ_ref[...], 1.0, 0.0).astype(BF16)

    def transpose(tab, first):
        for c in range(TAB // 128):
            hi, lo = split2(tab[c * 128:(c + 1) * 128, :].T)
            tt[0:128, c * 128:(c + 1) * 128] = hi
            tt[128:256, c * 128:(c + 1) * 128] = lo
        g = lax.dot_general(tt[...], tt[...], NT, preferred_element_type=F32)
        if first:
            gacc[...] = g
        else:
            gacc[...] += g

    own.wait()
    transpose(tab0, True)

    for copy in ent_copies:
        copy.wait_recv()

    xr = [lax.rem(x + rel, NX) for rel in range(NX)]
    for i in range(NZ):
        ent2[0, i] = ent[i]
        ent2[1, i] = pltpu.roll(ent[i], 64, 1)
    low = iota((1, 128), 1) < 64

    def full_row(i, c, rel):
        return ent[i, pl.ds(c * 8 + xr[rel], 1), :]

    def half_row(i, c, rel, d):
        return ent2[lax.rem(xr[rel] + d, 2), i, pl.ds(c * 8 + NX + lax.div(xr[rel], 2), 1), :]

    for rel in range(NX):
        for g in range(2):
            row = rel * 2 + g
            for t in range(4):
                idr[row:row + 1, t * 128:(t + 1) * 128] = full_row(4 * g + t, 0, rel)
            for t in range(2):
                a = 4 * g + 2 * t
                first, second = (a, a + 1) if rel % 2 == 0 else (a + 1, a)
                idr[row:row + 1, 512 + t * 128:640 + t * 128] = jnp.where(
                    low, half_row(first, 0, rel, 0), half_row(second, 0, rel, 1))

    ucode = (iota((U, 128), 0) + 1).astype(F32)
    for i in range(NZ):
        for t in range(KH):
            if t < NX:
                user, m = full_row(i, 1, t), full_row(i, 2, t)
            else:
                pair = 2 * (t - NX)
                first, second = (pair, pair + 1) if i % 2 == 0 else (pair + 1, pair)
                user = jnp.where(low, half_row(i, 1, first, 0), half_row(i, 1, second, 1))
                m = jnp.where(low, half_row(i, 2, first, 0), half_row(i, 2, second, 1))
            eq = user == ucode
            mw[i, :, t * 128:(t + 1) * 128] = jnp.where(eq, m * (1.0 / D), 0.0)
            mb[i, :, t * 128:(t + 1) * 128] = jnp.where(eq, (1.0 + m) * (1.0 / math.sqrt(D)), 0.0)

    def collect(rel, other):
        def group(g, carry):
            wanted = idr[pl.ds(rel * 2 + g, 1), :]
            item = iota((256, SLOTS), 0).astype(F32)
            acc = None
            for b in range(TAB // 256):
                hot = jnp.where(item == wanted - b * 256.0, 1.0, 0.0).astype(BF16)
                d = jnp.dot(tt[:, b * 256:(b + 1) * 256], hot, preferred_element_type=F32)
                acc = d if acc is None else acc + d
            for t in range(4):
                ft[4 * g + t, :, rel * 128:(rel + 1) * 128] = acc[:, t * 128:(t + 1) * 128].astype(BF16)
            for t in range(2):
                now = acc[:, 512 + t * 128:640 + t * 128]
                if other is None:
                    halves[2 * g + t] = now
                else:
                    then = halves[2 * g + t]
                    even, odd = (now, then) if rel % 2 == 0 else (then, now)
                    keep = iota((256, 128), 1) < 64
                    cols = slice((NX + rel // 2) * 128, (NX + rel // 2 + 1) * 128)
                    ft[4 * g + 2 * t, :, cols] = jnp.where(keep, even, odd).astype(BF16)
                    ft[4 * g + 2 * t + 1, :, cols] = jnp.where(keep, odd, even).astype(BF16)
            return carry

        lax.fori_loop(0, 2, group, 0)

    right[0].wait_recv()
    fwd_right.start()
    to_sib[0].start()
    left[1].wait_recv()
    fwd_left.start()
    to_sib[1].start()
    collect(0, None)
    left[0].wait_recv()
    to_sib[3].start()
    right[1].wait_recv()
    to_sib[2].start()
    for i in (1, 3):
        to_sib[i].wait_recv()
    transpose(tab1, False)
    collect(1, 0)
    for i in (0, 2):
        to_sib[i].wait_recv()
    transpose(tab3, False)
    fwd_right.wait_recv()
    to_sib[4].start()
    fwd_left.wait_recv()
    to_sib[5].start()
    collect(3, None)
    for i in (4, 5):
        to_sib[i].wait_recv()
    transpose(tab2, False)
    collect(2, 3)

    scale = 2.0 / ITEMS
    g = (gacc[0:128, 0:128] + gacc[0:128, 128:256] + gacc[128:256, 0:128] + gacc[128:256, 128:256]) * scale
    ghl = jnp.concatenate(split2(g), axis=0)
    for i in range(NZ):
        ft[i, :, SLOTS:SLOTS + 128] = ghl

    def fold(res):
        return res[0:U, 0:128] + res[0:U, 128:256] + res[U:2 * U, 0:128]

    def rhs_share(i):
        hi, lo = split2(mb[i])
        return fold(lax.dot_general(
            jnp.concatenate([hi, lo], axis=0), ft[i, :, 0:SLOTS], NT, preferred_element_type=F32))

    def project(i, hi, lo):
        lhs = jnp.concatenate(
            [jnp.concatenate([hi, hi], axis=1), jnp.concatenate([lo, jnp.zeros_like(lo)], axis=1)], axis=0)
        res = jnp.dot(lhs, ft[i, :, 0:SLOTS], preferred_element_type=F32)
        return res[0:U] + res[U:2 * U]

    def share(i, p):
        hi, lo = split2(p)
        yhi, ylo = split2(mw[i] * project(i, hi, lo))
        lhs = jnp.concatenate(
            [jnp.concatenate([yhi, hi], axis=1), jnp.concatenate([ylo, lo], axis=1)], axis=0)
        return fold(lax.dot_general(lhs, ft[i], NT, preferred_element_type=F32))

    def last_share(i, p):
        hi, lo = split2(p)
        proj = project(i, hi, lo)
        sq = mw[i] * proj * proj
        t = fold(lax.dot_general(
            jnp.concatenate([hi, lo], axis=0), ft[i, :, SLOTS:SLOTS + 128], NT, preferred_element_type=F32)) * p
        for kh in range(KH):
            t = t + sq[:, kh * 128:(kh + 1) * 128]
        block = lax.shift_right_logical(iota((8, 128), 1), 5)
        folded = jnp.zeros((8, 128), F32)
        for c in range(4):
            v = t[c * 8:(c + 1) * 8]
            v = v + pltpu.roll(v, 64, 1)
            v = v + pltpu.roll(v, 32, 1)
            folded = jnp.where(block == c, v, folded)
        return folded

    p_copies = {dz: remote(psend, pbuf.at[z], ps_sem.at[dz], pr_sem.at[dz], zpeer(dz)) for dz in ORDER}
    q_copies = {
        dz: remote(qsend.at[dz], qbuf.at[NZ - dz], qs_sem.at[dz], qr_sem.at[NZ - dz], zpeer(dz)) for dz in ORDER}
    t_copies = {
        dz: remote(qsend.at[dz, 0:8], qbuf.at[NZ - dz, 0:8], qs_sem.at[dz], qr_sem.at[NZ - dz], zpeer(dz))
        for dz in ORDER}

    def answer(group, fn, copies, rows):
        shares = [fn(lax.rem(z + dz, NZ), dz) for dz in group]
        for dz, value in zip(group, shares):
            qsend[dz, 0:rows] = value
            copies[dz].start()

    def collect_shares(total, copies, rows):
        for dz in ORDER:
            copies[dz].wait_recv()
        for dz in range(1, NZ):
            total = total + qbuf[dz, 0:rows]
        for dz in ORDER:
            copies[dz].wait_send()
        return total

    def exchange(fn, p, copies, rows):
        psend[...] = p
        for dz in FAR:
            p_copies[dz].start()
        total = fn(z, p)
        for group in GROUPS:
            for dz in group:
                p_copies[NZ - dz].wait_recv()
            answer(group, lambda i, dz: fn(i, pbuf[i]), copies, rows)
        total = collect_shares(total, copies, rows)
        for dz in ORDER:
            p_copies[dz].wait_send()
        return total

    answer((4, 3, 5), lambda i, dz: rhs_share(i), q_copies, U)
    answer((2, 6, 1, 7), lambda i, dz: rhs_share(i), q_copies, U)
    rhs = collect_shares(rhs_share(z), q_copies, U)

    def norm(v):
        return jnp.sum(v * v, axis=1, keepdims=True)

    def iterate(_, carry):
        sol, res, p, rr = carry
        q = p + exchange(share, p, q_copies, U)
        alpha = rr / jnp.sum(p * q, axis=1, keepdims=True)
        sol = sol + alpha * p
        res = res - alpha * q
        new = norm(res)
        return sol, res, res + (new / rr) * p, new

    carry = (jnp.zeros_like(rhs), rhs, rhs, norm(rhs))
    sol, res, p, rr = lax.fori_loop(0, ITERS - 1, iterate, carry)
    folded = exchange(last_share, p, t_copies, 8)
    block = lax.shift_right_logical(iota((8, 128), 1), 5)
    pq = norm(p) + jnp.concatenate(
        [jnp.sum(jnp.where(block == c, folded, 0.0), axis=1, keepdims=True) for c in range(4)], axis=0)
    sol = sol + (rr / pq) * p

    def group_rows(dy, c):
        return pl.ds(pl.multiple_of((lax.rem(y + dy, NY) * 2 + c) * U, U), U)

    gat[group_rows(0, core), :] = sol
    mine = gat.at[group_rows(0, core)]
    y_copies = [remote(mine, mine, ys_sem.at[dy], yr_sem.at[dy], ypeer(dy)) for dy in range(1, NY)]
    s_copies = [
        remote(gat.at[group_rows(dy, core)], gat.at[group_rows(dy, core)], ss_sem.at[dy], sr_sem.at[dy], sibling)
        for dy in range(NY)
    ]
    for copy in reversed(y_copies):
        copy.start()
    s_copies[0].start()
    for dy in (1, 7, 2, 6, 3, 5, 4):
        y_copies[NY - dy - 1].wait_recv()
        s_copies[dy].start()
    for copy in s_copies:
        copy.wait_recv()
    hml = jnp.concatenate(split3(gat[...]), axis=1)
    placed = jnp.dot(place[...], hml, preferred_element_type=F32)
    out_ref[...] = placed[:, 0:128] + placed[:, 128:256] + placed[:, 256:384]

    for copy in right + left + [fwd_right, fwd_left] + to_sib + ent_copies + y_copies + s_copies:
        copy.wait_send()


def per_device(item_table, neighbours, confidence, valid_counts, row_targets):
    dma = pltpu.SemaphoreType.DMA
    return pl.pallas_call(
        kernel,
        out_shape=jax.ShapeDtypeStruct((512, D), F32),
        in_specs=[pl.BlockSpec(memory_space=pltpu.HBM)] * 5,
        out_specs=pl.BlockSpec(memory_space=pltpu.VMEM),
        scratch_shapes=[
            pltpu.SMEM((U,), I32), pltpu.VMEM((U, K), I32), pltpu.VMEM((U, K), F32), pltpu.VMEM((1, 512), I32),
            pltpu.VMEM((TAB, D), F32), pltpu.VMEM((TAB, D), F32), pltpu.VMEM((TAB, D), F32), pltpu.VMEM((TAB, D), F32),
            pltpu.VMEM((U, K), I32), pltpu.VMEM((U, K), I32), pltpu.VMEM((6, U, K), F32),
            pltpu.VMEM((128, U * K), BF16), pltpu.VMEM((6 * 64, U * K), BF16),
            pltpu.VMEM((NZ, 24, 128), F32), pltpu.VMEM((NZ, 24, 128), F32), pltpu.VMEM((2, NZ, 24, 128), F32),
            pltpu.VMEM((2 * NX, SLOTS), F32), pltpu.VMEM((2 * D, TAB), BF16), pltpu.VMEM((4, 2 * D, 128), F32),
            pltpu.VMEM((NZ, 2 * D, SLOTS + 128), BF16),
            pltpu.VMEM((NZ, U, SLOTS), F32), pltpu.VMEM((NZ, U, SLOTS), F32), pltpu.VMEM((2 * D, 2 * D), F32),
            pltpu.VMEM((U, D), F32), pltpu.VMEM((NZ, U, D), F32),
            pltpu.VMEM((NZ, U, D), F32), pltpu.VMEM((NZ, U, D), F32),
            pltpu.VMEM((512, D), F32), pltpu.VMEM((512, 512), BF16),
            dma((4,)), dma, dma((4,)), dma((6,)), dma((2,)), dma((6,)), dma((6,)), dma((7,)), dma((7,)),
            dma((NZ,)), dma((NZ,)), dma((NZ,)), dma((NZ,)), dma((NY,)), dma((NY,)), dma((NY,)), dma((NY,)),
        ],
        compiler_params=pltpu.CompilerParams(
            collective_id=0, has_side_effects=True, vmem_limit_bytes=48 * 1024 * 1024),
    )(valid_counts, neighbours, confidence, row_targets.reshape(1, 512), item_table)


def solution(mesh):
    return jax.shard_map(
        per_device,
        mesh=mesh,
        in_specs=(
            P("shard", None),
            P(("replica", "shard"), None),
            P(("replica", "shard"), None),
            P(("replica", "shard")),
            P("shard"),
        ),
        out_specs=P("shard", None),
        check_vma=False,
    )
```

```python
import math

import jax
import jax.numpy as jnp
from jax import lax
from jax.experimental import pallas as pl
from jax.experimental.pallas import tpu as pltpu
from jax.sharding import PartitionSpec as P

ITERS = 4
NX, NZ, NY = 4, 8, 8
D = 128
K = 128
U = 32
TAB = 2048
ITEMS = 65536
CAP = 192
SLOTS = NX * CAP
KH = SLOTS // 128
MESH = pl.DeviceIdType.MESH
F32, BF16, I32 = jnp.float32, jnp.bfloat16, jnp.int32
ORDER = (1, 7, 2, 6, 3, 5, 4)
FAR = (4, 3, 5, 2, 6, 1, 7)
GROUPS = ((1, 7), (2, 6), (3, 5), (4,))
SENDS = {(1, 7): (), (2, 6): (), (3, 5): (), (4,): (4, 3, 5, 2, 6, 1, 7)}
NT = (((1,), (1,)), ((), ()))
TN = (((0,), (0,)), ((), ()))


def split2(v):
    hi = v.astype(BF16)
    lo = (v - hi.astype(F32)).astype(BF16)
    return hi, lo


def split3(v):
    hi = v.astype(BF16)
    rest = v - hi.astype(F32)
    mid = rest.astype(BF16)
    lo = (rest - mid.astype(F32)).astype(BF16)
    return hi, mid, lo


def iota(shape, dim):
    return lax.broadcasted_iota(I32, shape, dim)


def kernel(
    counts_hbm, ids_hbm, conf_hbm, targ_hbm, table,
    out_ref,
    counts, ids_ref, conf_ref, targ_ref,
    tab0, tab1, tab2, tab3, code_s, kl_s, val_s, a_s, b_s, ent_send, ent, ent2, idr, tt, halves, ft, mw, mb, gacc,
    psend, pbuf, qsend, qbuf, gat, place,
    in_sem, own_sem, tx_sem, trx_sem, tfwd_sem, ts_sem, tsr_sem, es_sem, er_sem, ps_sem, pr_sem, qs_sem, qr_sem,
    ys_sem, yr_sem, ss_sem, sr_sem,
):
    r = lax.axis_index("replica")
    s = lax.axis_index("shard")
    z, x = lax.div(s, NX), lax.rem(s, NX)
    y, core = lax.div(r, 2), lax.rem(r, 2)

    def zpeer(dz):
        return (r, lax.rem(z + dz, NZ) * NX + x)

    def xpeer(dx):
        return (r, z * NX + lax.rem(x + dx, NX))

    def ypeer(dy):
        return (lax.rem(y + dy, NY) * 2 + core, s)

    sibling = (y * 2 + 1 - core, s)

    loads = [
        pltpu.make_async_copy(src, dst, in_sem.at[i])
        for i, (src, dst) in enumerate(
            [(ids_hbm, ids_ref), (counts_hbm, counts), (conf_hbm, conf_ref), (targ_hbm, targ_ref)])
    ]
    own = pltpu.make_async_copy(table, tab0, own_sem)
    for load in loads:
        load.start()
    own.start()

    barrier = pltpu.get_barrier_semaphore()
    peers = [zpeer(dz) for dz in range(1, NZ)] + [xpeer(1), xpeer(3), sibling]
    peers += [ypeer(dy) for dy in range(1, NY)]
    for peer in peers:
        pl.semaphore_signal(barrier, inc=1, device_id=peer, device_id_type=MESH)

    half = TAB // 2
    piece = half // 2

    def rows_of(c):
        return pl.ds(pl.multiple_of(core * half + c * piece, piece), piece)

    def remote(src, dst, send, recv, peer):
        return pltpu.make_async_remote_copy(
            src_ref=src, dst_ref=dst, send_sem=send, recv_sem=recv, device_id=peer, device_id_type=MESH)

    right = [remote(table.at[rows_of(c)], tab3.at[rows_of(c)], tx_sem.at[c], trx_sem.at[c], xpeer(1)) for c in range(2)]
    left = [remote(table.at[rows_of(c)], tab1.at[rows_of(c)], tx_sem.at[2 + c], trx_sem.at[2 + c], xpeer(3)) for c in range(2)]
    fwd_right = remote(tab3.at[rows_of(0)], tab2.at[rows_of(0)], tfwd_sem.at[0], trx_sem.at[4], xpeer(1))
    fwd_left = remote(tab1.at[rows_of(1)], tab2.at[rows_of(1)], tfwd_sem.at[1], trx_sem.at[5], xpeer(3))
    arrivals = [(tab3, 0), (tab1, 1), (tab3, 1), (tab1, 0), (tab2, 0), (tab2, 1)]
    to_sib = [
        remote(t.at[rows_of(c)], t.at[rows_of(c)], ts_sem.at[i], tsr_sem.at[i], sibling)
        for i, (t, c) in enumerate(arrivals)
    ]

    for load in loads[:3]:
        load.wait()
    ids = ids_ref[...]
    owner = lax.shift_right_logical(ids, 11)
    local = ids & (TAB - 1)
    rowi = iota((U, K), 0)
    lane = iota((U, K), 1)
    cnt = jnp.zeros((U, K), I32)
    for u in range(U):
        cnt = jnp.where(rowi == u, counts[u], cnt)
    used = lane < cnt
    key = jnp.where(used, owner, -1)
    e_all = jnp.concatenate(
        [jnp.where(key == o, 1.0, 0.0).astype(BF16) for o in range(NX * NZ)], axis=0)
    br, bc = iota((256, 256), 0), iota((256, 256), 1)
    lower = jnp.where((lax.shift_right_logical(br, 5) == lax.shift_right_logical(bc, 5)) & (bc < br), 1.0, 0.0).astype(BF16)
    x_all = jnp.concatenate(
        [jnp.dot(lower, e_all[i * 256:(i + 1) * 256], preferred_element_type=F32).astype(BF16) for i in range(4)], axis=0)
    tr, tc = iota((256, 128), 0), iota((256, 128), 1)
    tri = jnp.where((tr >= 128) | (tr < tc), 1.0, 0.0).astype(BF16)
    pos_all = jnp.dot(jnp.concatenate([e_all, x_all], axis=1), tri, preferred_element_type=F32)
    pos = jnp.zeros((U, K), F32)
    for o in range(NX * NZ):
        pos = jnp.where(key == o, pos_all[o * U:(o + 1) * U], pos)
    pos = pos.astype(I32)
    ox = owner & (NX - 1)
    full = pos < 128
    part = jnp.where(full, lax.shift_right_logical(pos, 6), ox & 1)
    row = jnp.where(full, ox, NX + lax.shift_right_logical(ox, 1))
    code_s[...] = jnp.where(used, part * 64 + lax.shift_right_logical(owner, 2) * 8 + row, -1)
    kl_s[...] = pos & 63
    m1, m2 = split2(conf_ref[...])
    val_s[0] = (local & 0xFF).astype(F32)
    val_s[1] = (rowi * 8 + lax.shift_right_logical(local, 8)).astype(F32)
    val_s[2] = m1.astype(F32)
    val_s[3] = m2.astype(F32)
    sub = iota((128, 128), 0)

    def build(u, carry):
        cols = pl.ds(pl.multiple_of(u * 128, 128), 128)
        a_s[:, cols] = jnp.where(sub == code_s[pl.ds(u, 1), :], 1.0, 0.0).astype(BF16)
        hot = sub[0:64] == kl_s[pl.ds(u, 1), :]
        for c in range(4):
            b_s[c * 64:(c + 1) * 64, cols] = jnp.where(hot, val_s[c, pl.ds(u, 1), :], 0.0).astype(BF16)
        return carry

    lax.fori_loop(0, U, build, 0)
    packed = lax.dot_general(b_s[...], a_s[...], NT, preferred_element_type=F32)

    def tiles(v):
        return jnp.concatenate([v[:, 0:64], v[:, 64:128]], axis=0).T.reshape(NZ, 8, 128)

    coded = packed[64:128].astype(I32)
    ent_send[:, 0:8, :] = tiles(packed[0:64] + ((coded & 7) * 256).astype(F32))
    ent_send[:, 8:16, :] = tiles(lax.shift_right_logical(coded, 3).astype(F32))
    ent_send[:, 16:24, :] = tiles(packed[128:192] + packed[192:256])
    ent[z] = ent_send[z]

    pl.semaphore_wait(barrier, len(peers))
    ent_copies = [
        remote(ent_send.at[lax.rem(z + dz, NZ)], ent.at[z], es_sem.at[i], er_sem.at[i], zpeer(dz))
        for i, dz in enumerate(ORDER)
    ]
    for copy in reversed(ent_copies):
        copy.start()
    right[0].start()
    left[1].start()
    right[1].start()
    left[0].start()

    loads[3].wait()
    place[...] = jnp.where(iota((512, 512), 0) == targ_ref[...], 1.0, 0.0).astype(BF16)

    def transpose(tab, first):
        for c in range(TAB // 128):
            hi, lo = split2(tab[c * 128:(c + 1) * 128, :].T)
            tt[0:128, c * 128:(c + 1) * 128] = hi
            tt[128:256, c * 128:(c + 1) * 128] = lo
        g = lax.dot_general(tt[...], tt[...], NT, preferred_element_type=F32)
        if first:
            gacc[...] = g
        else:
            gacc[...] += g

    own.wait()
    transpose(tab0, True)

    for copy in ent_copies:
        copy.wait_recv()

    xr = [lax.rem(x + rel, NX) for rel in range(NX)]
    for i in range(NZ):
        ent2[0, i] = ent[i]
        ent2[1, i] = pltpu.roll(ent[i], 64, 1)
    low = iota((1, 128), 1) < 64

    def full_row(i, c, rel):
        return ent[i, pl.ds(c * 8 + xr[rel], 1), :]

    def half_row(i, c, rel, d):
        return ent2[lax.rem(xr[rel] + d, 2), i, pl.ds(c * 8 + NX + lax.div(xr[rel], 2), 1), :]

    for rel in range(NX):
        for g in range(2):
            row = rel * 2 + g
            for t in range(4):
                idr[row:row + 1, t * 128:(t + 1) * 128] = full_row(4 * g + t, 0, rel)
            for t in range(2):
                a = 4 * g + 2 * t
                first, second = (a, a + 1) if rel % 2 == 0 else (a + 1, a)
                idr[row:row + 1, 512 + t * 128:640 + t * 128] = jnp.where(
                    low, half_row(first, 0, rel, 0), half_row(second, 0, rel, 1))

    ucode = iota((U, 128), 0).astype(F32)
    for i in range(NZ):
        for t in range(KH):
            if t < NX:
                user, m = full_row(i, 1, t), full_row(i, 2, t)
            else:
                pair = 2 * (t - NX)
                first, second = (pair, pair + 1) if i % 2 == 0 else (pair + 1, pair)
                user = jnp.where(low, half_row(i, 1, first, 0), half_row(i, 1, second, 1))
                m = jnp.where(low, half_row(i, 2, first, 0), half_row(i, 2, second, 1))
            eq = user == ucode
            mw[i, :, t * 128:(t + 1) * 128] = jnp.where(eq, m * (1.0 / D), 0.0)
            mb[i, :, t * 128:(t + 1) * 128] = jnp.where(eq & (m > 0.0), (1.0 + m) * (1.0 / math.sqrt(D)), 0.0)

    def collect(rel, other):
        def group(g, carry):
            wanted = idr[pl.ds(rel * 2 + g, 1), :]
            item = iota((256, SLOTS), 0).astype(F32)
            acc = None
            for b in range(TAB // 256):
                hot = jnp.where(item == wanted - b * 256.0, 1.0, 0.0).astype(BF16)
                d = jnp.dot(tt[:, b * 256:(b + 1) * 256], hot, preferred_element_type=F32)
                acc = d if acc is None else acc + d
            for t in range(4):
                ft[4 * g + t, :, rel * 128:(rel + 1) * 128] = acc[:, t * 128:(t + 1) * 128].astype(BF16)
            for t in range(2):
                now = acc[:, 512 + t * 128:640 + t * 128]
                if other is None:
                    halves[2 * g + t] = now
                else:
                    then = halves[2 * g + t]
                    even, odd = (now, then) if rel % 2 == 0 else (then, now)
                    keep = iota((256, 128), 1) < 64
                    cols = slice((NX + rel // 2) * 128, (NX + rel // 2 + 1) * 128)
                    ft[4 * g + 2 * t, :, cols] = jnp.where(keep, even, odd).astype(BF16)
                    ft[4 * g + 2 * t + 1, :, cols] = jnp.where(keep, odd, even).astype(BF16)
            return carry

        lax.fori_loop(0, 2, group, 0)

    right[0].wait_recv()
    fwd_right.start()
    to_sib[0].start()
    left[1].wait_recv()
    fwd_left.start()
    to_sib[1].start()
    collect(0, None)
    left[0].wait_recv()
    to_sib[3].start()
    right[1].wait_recv()
    to_sib[2].start()
    for i in (1, 3):
        to_sib[i].wait_recv()
    transpose(tab1, False)
    collect(1, 0)
    for i in (0, 2):
        to_sib[i].wait_recv()
    transpose(tab3, False)
    fwd_right.wait_recv()
    to_sib[4].start()
    fwd_left.wait_recv()
    to_sib[5].start()
    collect(3, None)
    for i in (4, 5):
        to_sib[i].wait_recv()
    transpose(tab2, False)
    collect(2, 3)

    def fold(res):
        return res[0:U, 0:128] + res[0:U, 128:256] + res[U:2 * U, 0:128]

    def rhs_share(i):
        hi, lo = split2(mb[i])
        return fold(lax.dot_general(
            jnp.concatenate([hi, lo], axis=0), ft[i, :, 0:SLOTS], NT, preferred_element_type=F32))

    def project(i, hi, lo):
        lhs = jnp.concatenate(
            [jnp.concatenate([hi, hi], axis=1), jnp.concatenate([lo, jnp.zeros_like(lo)], axis=1)], axis=0)
        res = jnp.dot(lhs, ft[i, :, 0:SLOTS], preferred_element_type=F32)
        return res[0:U] + res[U:2 * U]

    def share(i, p):
        hi, lo = split2(p)
        yhi, ylo = split2(mw[i] * project(i, hi, lo))
        lhs = jnp.concatenate(
            [jnp.concatenate([yhi, hi], axis=1), jnp.concatenate([ylo, lo], axis=1)], axis=0)
        return fold(lax.dot_general(lhs, ft[i], NT, preferred_element_type=F32))

    def last_share(i, p):
        hi, lo = split2(p)
        proj = project(i, hi, lo)
        sq = mw[i] * proj * proj
        t = fold(lax.dot_general(
            jnp.concatenate([hi, lo], axis=0), ft[i, :, SLOTS:SLOTS + 128], NT, preferred_element_type=F32)) * p
        for kh in range(KH):
            t = t + sq[:, kh * 128:(kh + 1) * 128]
        block = lax.shift_right_logical(iota((8, 128), 1), 5)
        folded = jnp.zeros((8, 128), F32)
        for c in range(4):
            v = t[c * 8:(c + 1) * 8]
            v = v + pltpu.roll(v, 64, 1)
            v = v + pltpu.roll(v, 32, 1)
            folded = jnp.where(block == c, v, folded)
        return folded

    p_copies = {dz: remote(psend, pbuf.at[z], ps_sem.at[dz], pr_sem.at[dz], zpeer(dz)) for dz in ORDER}
    q_copies = {
        dz: remote(qsend.at[dz], qbuf.at[NZ - dz], qs_sem.at[dz], qr_sem.at[NZ - dz], zpeer(dz)) for dz in ORDER}
    t_copies = {
        dz: remote(qsend.at[dz, 0:8], qbuf.at[NZ - dz, 0:8], qs_sem.at[dz], qr_sem.at[NZ - dz], zpeer(dz))
        for dz in ORDER}

    def answer(group, fn, rows):
        shares = [fn(lax.rem(z + dz, NZ), dz) for dz in group]
        for dz, value in zip(group, shares):
            qsend[dz, 0:rows] = value

    def collect_shares(total, copies, rows):
        for dz in ORDER:
            copies[dz].wait_recv()
        for dz in range(1, NZ):
            total = total + qbuf[dz, 0:rows]
        for dz in ORDER:
            copies[dz].wait_send()
        return total

    def exchange(fn, p, copies, rows):
        psend[...] = p
        for dz in FAR:
            p_copies[dz].start()
        total = fn(z, p)
        for group in GROUPS:
            for dz in group:
                p_copies[NZ - dz].wait_recv()
            answer(group, lambda i, dz: fn(i, pbuf[i]), rows)
            for dz in SENDS[group]:
                copies[dz].start()
        total = collect_shares(total, copies, rows)
        for dz in ORDER:
            p_copies[dz].wait_send()
        return total

    for group in ((4, 3, 5), (2, 6, 1, 7)):
        answer(group, lambda i, dz: rhs_share(i), U)
        for dz in group:
            q_copies[dz].start()
    scale = 2.0 / ITEMS
    g = (gacc[0:128, 0:128] + gacc[0:128, 128:256] + gacc[128:256, 0:128] + gacc[128:256, 128:256]) * scale
    ghl = jnp.concatenate(split2(g), axis=0)
    for i in range(NZ):
        ft[i, :, SLOTS:SLOTS + 128] = ghl
    rhs = collect_shares(rhs_share(z), q_copies, U)

    def norm(v):
        return jnp.sum(v * v, axis=1, keepdims=True)

    def iterate(_, carry):
        sol, res, p, rr = carry
        q = p + exchange(share, p, q_copies, U)
        alpha = rr / jnp.sum(p * q, axis=1, keepdims=True)
        sol = sol + alpha * p
        res = res - alpha * q
        new = norm(res)
        return sol, res, res + (new / rr) * p, new

    carry = (jnp.zeros_like(rhs), rhs, rhs, norm(rhs))
    sol, res, p, rr = lax.fori_loop(0, ITERS - 1, iterate, carry)
    folded = exchange(last_share, p, t_copies, 8)
    block = lax.shift_right_logical(iota((8, 128), 1), 5)
    pq = norm(p) + jnp.concatenate(
        [jnp.sum(jnp.where(block == c, folded, 0.0), axis=1, keepdims=True) for c in range(4)], axis=0)
    sol = sol + (rr / pq) * p

    def group_rows(dy, c):
        return pl.ds(pl.multiple_of((lax.rem(y + dy, NY) * 2 + c) * U, U), U)

    gat[group_rows(0, core), :] = sol
    mine = gat.at[group_rows(0, core)]
    y_copies = [remote(mine, mine, ys_sem.at[dy], yr_sem.at[dy], ypeer(dy)) for dy in range(1, NY)]
    s_copies = [
        remote(gat.at[group_rows(dy, core)], gat.at[group_rows(dy, core)], ss_sem.at[dy], sr_sem.at[dy], sibling)
        for dy in range(NY)
    ]
    for copy in reversed(y_copies):
        copy.start()
    s_copies[0].start()
    for dy in (1, 7, 2, 6, 3, 5, 4):
        y_copies[NY - dy - 1].wait_recv()
        s_copies[dy].start()
    for copy in s_copies:
        copy.wait_recv()
    hml = jnp.concatenate(split3(gat[...]), axis=1)
    placed = jnp.dot(place[...], hml, preferred_element_type=F32)
    out_ref[...] = placed[:, 0:128] + placed[:, 128:256] + placed[:, 256:384]

    for copy in right + left + [fwd_right, fwd_left] + to_sib + ent_copies + y_copies + s_copies:
        copy.wait_send()


def per_device(item_table, neighbours, confidence, valid_counts, row_targets):
    dma = pltpu.SemaphoreType.DMA
    return pl.pallas_call(
        kernel,
        out_shape=jax.ShapeDtypeStruct((512, D), F32),
        in_specs=[pl.BlockSpec(memory_space=pltpu.HBM)] * 5,
        out_specs=pl.BlockSpec(memory_space=pltpu.VMEM),
        scratch_shapes=[
            pltpu.SMEM((U,), I32), pltpu.VMEM((U, K), I32), pltpu.VMEM((U, K), F32), pltpu.VMEM((1, 512), I32),
            pltpu.VMEM((TAB, D), F32), pltpu.VMEM((TAB, D), F32), pltpu.VMEM((TAB, D), F32), pltpu.VMEM((TAB, D), F32),
            pltpu.VMEM((U, K), I32), pltpu.VMEM((U, K), I32), pltpu.VMEM((4, U, K), F32),
            pltpu.VMEM((128, U * K), BF16), pltpu.VMEM((4 * 64, U * K), BF16),
            pltpu.VMEM((NZ, 24, 128), F32), pltpu.VMEM((NZ, 24, 128), F32), pltpu.VMEM((2, NZ, 24, 128), F32),
            pltpu.VMEM((2 * NX, SLOTS), F32), pltpu.VMEM((2 * D, TAB), BF16), pltpu.VMEM((4, 2 * D, 128), F32),
            pltpu.VMEM((NZ, 2 * D, SLOTS + 128), BF16),
            pltpu.VMEM((NZ, U, SLOTS), F32), pltpu.VMEM((NZ, U, SLOTS), F32), pltpu.VMEM((2 * D, 2 * D), F32),
            pltpu.VMEM((U, D), F32), pltpu.VMEM((NZ, U, D), F32),
            pltpu.VMEM((NZ, U, D), F32), pltpu.VMEM((NZ, U, D), F32),
            pltpu.VMEM((512, D), F32), pltpu.VMEM((512, 512), BF16),
            dma((4,)), dma, dma((4,)), dma((6,)), dma((2,)), dma((6,)), dma((6,)), dma((7,)), dma((7,)),
            dma((NZ,)), dma((NZ,)), dma((NZ,)), dma((NZ,)), dma((NY,)), dma((NY,)), dma((NY,)), dma((NY,)),
        ],
        compiler_params=pltpu.CompilerParams(
            collective_id=0, has_side_effects=True, vmem_limit_bytes=60 * 1024 * 1024),
    )(valid_counts, neighbours, confidence, row_targets.reshape(1, 512), item_table)


def solution(mesh):
    return jax.shard_map(
        per_device,
        mesh=mesh,
        in_specs=(
            P("shard", None),
            P(("replica", "shard"), None),
            P(("replica", "shard"), None),
            P(("replica", "shard")),
            P("shard"),
        ),
        out_specs=P("shard", None),
        check_vma=False,
    )
```

```python
import math

import jax
import jax.numpy as jnp
from jax import lax
from jax.experimental import pallas as pl
from jax.experimental.pallas import tpu as pltpu
from jax.sharding import PartitionSpec as P

ITERS = 4
NX, NZ, NY = 4, 8, 8
D = 128
K = 128
U = 32
TAB = 2048
ITEMS = 65536
CAP = 192
SLOTS = NX * CAP
KH = SLOTS // 128
MESH = pl.DeviceIdType.MESH
F32, BF16, I32 = jnp.float32, jnp.bfloat16, jnp.int32
ORDER = (1, 7, 2, 6, 3, 5, 4)
FAR = (4, 3, 5, 2, 6, 1, 7)
GROUPS = ((1, 7), (2, 6), (3, 5), (4,))
SENDS = {(1, 7): (), (2, 6): (), (3, 5): (), (4,): (4, 3, 5, 2, 6, 1, 7)}
NT = (((1,), (1,)), ((), ()))
TN = (((0,), (0,)), ((), ()))


def split2(v):
    hi = v.astype(BF16)
    lo = (v - hi.astype(F32)).astype(BF16)
    return hi, lo


def split3(v):
    hi = v.astype(BF16)
    rest = v - hi.astype(F32)
    mid = rest.astype(BF16)
    lo = (rest - mid.astype(F32)).astype(BF16)
    return hi, mid, lo


def iota(shape, dim):
    return lax.broadcasted_iota(I32, shape, dim)


def kernel(
    counts_hbm, ids_hbm, conf_hbm, targ_hbm, table,
    out_ref,
    counts, ids_ref, conf_ref, targ_ref,
    tab0, tab1, tab2, tab3, code_s, kl_s, val_s, a_s, b_s, ent_send, ent, ent2, idr, tt, halves, ft, fn, mw, mb, gacc,
    psend, pbuf, qsend, qbuf, gat, place,
    in_sem, own_sem, tx_sem, trx_sem, tfwd_sem, ts_sem, tsr_sem, es_sem, er_sem, ps_sem, pr_sem, qs_sem, qr_sem,
    ys_sem, yr_sem, ss_sem, sr_sem,
):
    r = lax.axis_index("replica")
    s = lax.axis_index("shard")
    z, x = lax.div(s, NX), lax.rem(s, NX)
    y, core = lax.div(r, 2), lax.rem(r, 2)

    def zpeer(dz):
        return (r, lax.rem(z + dz, NZ) * NX + x)

    def xpeer(dx):
        return (r, z * NX + lax.rem(x + dx, NX))

    def ypeer(dy):
        return (lax.rem(y + dy, NY) * 2 + core, s)

    sibling = (y * 2 + 1 - core, s)

    loads = [
        pltpu.make_async_copy(src, dst, in_sem.at[i])
        for i, (src, dst) in enumerate(
            [(ids_hbm, ids_ref), (counts_hbm, counts), (conf_hbm, conf_ref), (targ_hbm, targ_ref)])
    ]
    own = pltpu.make_async_copy(table, tab0, own_sem)
    for load in loads:
        load.start()
    own.start()

    barrier = pltpu.get_barrier_semaphore()
    peers = [zpeer(dz) for dz in range(1, NZ)] + [xpeer(1), xpeer(3), sibling]
    peers += [ypeer(dy) for dy in range(1, NY)]
    for peer in peers:
        pl.semaphore_signal(barrier, inc=1, device_id=peer, device_id_type=MESH)

    half = TAB // 2
    piece = half // 2

    def rows_of(c):
        return pl.ds(pl.multiple_of(core * half + c * piece, piece), piece)

    def remote(src, dst, send, recv, peer):
        return pltpu.make_async_remote_copy(
            src_ref=src, dst_ref=dst, send_sem=send, recv_sem=recv, device_id=peer, device_id_type=MESH)

    right = [remote(table.at[rows_of(c)], tab3.at[rows_of(c)], tx_sem.at[c], trx_sem.at[c], xpeer(1)) for c in range(2)]
    left = [remote(table.at[rows_of(c)], tab1.at[rows_of(c)], tx_sem.at[2 + c], trx_sem.at[2 + c], xpeer(3)) for c in range(2)]
    fwd_right = remote(tab3.at[rows_of(0)], tab2.at[rows_of(0)], tfwd_sem.at[0], trx_sem.at[4], xpeer(1))
    fwd_left = remote(tab1.at[rows_of(1)], tab2.at[rows_of(1)], tfwd_sem.at[1], trx_sem.at[5], xpeer(3))
    arrivals = [(tab3, 0), (tab1, 1), (tab3, 1), (tab1, 0), (tab2, 0), (tab2, 1)]
    to_sib = [
        remote(t.at[rows_of(c)], t.at[rows_of(c)], ts_sem.at[i], tsr_sem.at[i], sibling)
        for i, (t, c) in enumerate(arrivals)
    ]

    for load in loads[:3]:
        load.wait()
    ids = ids_ref[...]
    owner = lax.shift_right_logical(ids, 11)
    local = ids & (TAB - 1)
    rowi = iota((U, K), 0)
    lane = iota((U, K), 1)
    cnt = jnp.zeros((U, K), I32)
    for u in range(U):
        cnt = jnp.where(rowi == u, counts[u], cnt)
    used = lane < cnt
    key = jnp.where(used, owner, -1)
    e_all = jnp.concatenate(
        [jnp.where(key == o, 1.0, 0.0).astype(BF16) for o in range(NX * NZ)], axis=0)
    br, bc = iota((256, 256), 0), iota((256, 256), 1)
    lower = jnp.where((lax.shift_right_logical(br, 5) == lax.shift_right_logical(bc, 5)) & (bc < br), 1.0, 0.0).astype(BF16)
    x_all = jnp.concatenate(
        [jnp.dot(lower, e_all[i * 256:(i + 1) * 256], preferred_element_type=F32).astype(BF16) for i in range(4)], axis=0)
    tr, tc = iota((256, 128), 0), iota((256, 128), 1)
    tri = jnp.where((tr >= 128) | (tr < tc), 1.0, 0.0).astype(BF16)
    pos_all = jnp.dot(jnp.concatenate([e_all, x_all], axis=1), tri, preferred_element_type=F32)
    pos = jnp.zeros((U, K), F32)
    for o in range(NX * NZ):
        pos = jnp.where(key == o, pos_all[o * U:(o + 1) * U], pos)
    pos = pos.astype(I32)
    ox = owner & (NX - 1)
    full = pos < 128
    part = jnp.where(full, lax.shift_right_logical(pos, 6), ox & 1)
    row = jnp.where(full, ox, NX + lax.shift_right_logical(ox, 1))
    code_s[...] = jnp.where(used, part * 64 + lax.shift_right_logical(owner, 2) * 8 + row, -1)
    kl_s[...] = pos & 63
    m1, m2 = split2(conf_ref[...])
    val_s[0] = (local & 0xFF).astype(F32)
    val_s[1] = (rowi * 8 + lax.shift_right_logical(local, 8)).astype(F32)
    val_s[2] = m1.astype(F32)
    val_s[3] = m2.astype(F32)
    sub = iota((128, 128), 0)

    def build(u, carry):
        cols = pl.ds(pl.multiple_of(u * 128, 128), 128)
        a_s[:, cols] = jnp.where(sub == code_s[pl.ds(u, 1), :], 1.0, 0.0).astype(BF16)
        hot = sub[0:64] == kl_s[pl.ds(u, 1), :]
        for c in range(4):
            b_s[c * 64:(c + 1) * 64, cols] = jnp.where(hot, val_s[c, pl.ds(u, 1), :], 0.0).astype(BF16)
        return carry

    lax.fori_loop(0, U, build, 0)
    packed = lax.dot_general(b_s[...], a_s[...], NT, preferred_element_type=F32)

    def tiles(v):
        return jnp.concatenate([v[:, 0:64], v[:, 64:128]], axis=0).T.reshape(NZ, 8, 128)

    coded = packed[64:128].astype(I32)
    ent_send[:, 0:8, :] = tiles(packed[0:64] + ((coded & 7) * 256).astype(F32))
    ent_send[:, 8:16, :] = tiles(lax.shift_right_logical(coded, 3).astype(F32))
    ent_send[:, 16:24, :] = tiles(packed[128:192] + packed[192:256])
    ent[z] = ent_send[z]

    pl.semaphore_wait(barrier, len(peers))
    ent_copies = [
        remote(ent_send.at[lax.rem(z + dz, NZ)], ent.at[z], es_sem.at[i], er_sem.at[i], zpeer(dz))
        for i, dz in enumerate(ORDER)
    ]
    for copy in reversed(ent_copies):
        copy.start()
    right[0].start()
    left[1].start()
    right[1].start()
    left[0].start()

    loads[3].wait()
    place[...] = jnp.where(iota((512, 512), 0) == targ_ref[...], 1.0, 0.0).astype(BF16)

    def add_gram(first):
        g = lax.dot_general(tt[...], tt[...], NT, preferred_element_type=F32)
        gacc[...] = g if first else gacc[...] + g

    def transpose(tab, first, last=False):
        for c in range(TAB // 128):
            hi, lo = split2(tab[c * 128:(c + 1) * 128, :].T)
            tt[0:128, c * 128:(c + 1) * 128] = hi
            tt[128:256, c * 128:(c + 1) * 128] = lo
        if not last:
            add_gram(first)

    own.wait()
    transpose(tab0, True)

    for copy in ent_copies:
        copy.wait_recv()

    xr = [lax.rem(x + rel, NX) for rel in range(NX)]
    for i in range(NZ):
        ent2[0, i] = ent[i]
        ent2[1, i] = pltpu.roll(ent[i], 64, 1)
    low = iota((1, 128), 1) < 64

    def full_row(i, c, rel):
        return ent[i, pl.ds(c * 8 + xr[rel], 1), :]

    def half_row(i, c, rel, d):
        return ent2[lax.rem(xr[rel] + d, 2), i, pl.ds(c * 8 + NX + lax.div(xr[rel], 2), 1), :]

    for rel in range(NX):
        for g in range(2):
            row = rel * 2 + g
            for t in range(4):
                idr[row:row + 1, t * 128:(t + 1) * 128] = full_row(4 * g + t, 0, rel)
            for t in range(2):
                a = 4 * g + 2 * t
                first, second = (a, a + 1) if rel % 2 == 0 else (a + 1, a)
                idr[row:row + 1, 512 + t * 128:640 + t * 128] = jnp.where(
                    low, half_row(first, 0, rel, 0), half_row(second, 0, rel, 1))

    ucode = iota((U, 128), 0).astype(F32)
    for i in range(NZ):
        for t in range(KH):
            if t < NX:
                user, m = full_row(i, 1, t), full_row(i, 2, t)
            else:
                pair = 2 * (t - NX)
                first, second = (pair, pair + 1) if i % 2 == 0 else (pair + 1, pair)
                user = jnp.where(low, half_row(i, 1, first, 0), half_row(i, 1, second, 1))
                m = jnp.where(low, half_row(i, 2, first, 0), half_row(i, 2, second, 1))
            eq = user == ucode
            mw[i, :, t * 128:(t + 1) * 128] = jnp.where(eq, m * (1.0 / D), 0.0)
            mb[i, :, t * 128:(t + 1) * 128] = jnp.where(eq & (m > 0.0), (1.0 + m) * (1.0 / math.sqrt(D)), 0.0)

    def collect(rel, other):
        def group(g, carry):
            wanted = idr[pl.ds(rel * 2 + g, 1), :]
            item = iota((256, SLOTS), 0).astype(F32)
            acc = None
            for b in range(TAB // 256):
                hot = jnp.where(item == wanted - b * 256.0, 1.0, 0.0).astype(BF16)
                d = jnp.dot(tt[:, b * 256:(b + 1) * 256], hot, preferred_element_type=F32)
                acc = d if acc is None else acc + d
            for t in range(4):
                ft[4 * g + t, :, rel * 128:(rel + 1) * 128] = acc[:, t * 128:(t + 1) * 128].astype(BF16)
            for t in range(2):
                now = acc[:, 512 + t * 128:640 + t * 128]
                if other is None:
                    halves[2 * g + t] = now
                else:
                    then = halves[2 * g + t]
                    even, odd = (now, then) if rel % 2 == 0 else (then, now)
                    keep = iota((256, 128), 1) < 64
                    cols = slice((NX + rel // 2) * 128, (NX + rel // 2 + 1) * 128)
                    ft[4 * g + 2 * t, :, cols] = jnp.where(keep, even, odd).astype(BF16)
                    ft[4 * g + 2 * t + 1, :, cols] = jnp.where(keep, odd, even).astype(BF16)
            return carry

        lax.fori_loop(0, 2, group, 0)

    right[0].wait_recv()
    fwd_right.start()
    to_sib[0].start()
    left[1].wait_recv()
    fwd_left.start()
    to_sib[1].start()
    collect(0, None)
    left[0].wait_recv()
    to_sib[3].start()
    right[1].wait_recv()
    to_sib[2].start()
    for i in (1, 3):
        to_sib[i].wait_recv()
    transpose(tab1, False)
    collect(1, 0)
    for i in (0, 2):
        to_sib[i].wait_recv()
    transpose(tab3, False)
    fwd_right.wait_recv()
    to_sib[4].start()
    fwd_left.wait_recv()
    to_sib[5].start()
    collect(3, None)
    for i in (4, 5):
        to_sib[i].wait_recv()
    transpose(tab2, False, True)
    collect(2, 3)

    def fold(res):
        return res[0:U, 0:128] + res[0:U, 128:256] + res[U:2 * U, 0:128]

    def rhs_share(i):
        hi, lo = split2(mb[i])
        return fold(lax.dot_general(
            jnp.concatenate([hi, lo], axis=0), ft[i], NT, preferred_element_type=F32))

    def project(i, hi, lo):
        lhs = jnp.concatenate(
            [jnp.concatenate([hi, hi], axis=1), jnp.concatenate([lo, jnp.zeros_like(lo)], axis=1)], axis=0)
        res = jnp.dot(lhs, ft[i], preferred_element_type=F32)
        return res[0:U] + res[U:2 * U]

    def share(i, p):
        hi, lo = split2(p)
        yhi, ylo = split2(mw[i] * project(i, hi, lo))
        lhs = jnp.concatenate(
            [jnp.concatenate([yhi, hi], axis=1), jnp.concatenate([ylo, lo], axis=1)], axis=0)
        return fold(jnp.dot(lhs, fn[i], preferred_element_type=F32))

    def last_share(i, p):
        hi, lo = split2(p)
        proj = project(i, hi, lo)
        sq = mw[i] * proj * proj
        t = fold(jnp.dot(
            jnp.concatenate([hi, lo], axis=0), fn[i, SLOTS:SLOTS + 128, :], preferred_element_type=F32)) * p
        for kh in range(KH):
            t = t + sq[:, kh * 128:(kh + 1) * 128]
        block = lax.shift_right_logical(iota((8, 128), 1), 5)
        folded = jnp.zeros((8, 128), F32)
        for c in range(4):
            v = t[c * 8:(c + 1) * 8]
            v = v + pltpu.roll(v, 64, 1)
            v = v + pltpu.roll(v, 32, 1)
            folded = jnp.where(block == c, v, folded)
        return folded

    p_copies = {dz: remote(psend, pbuf.at[z], ps_sem.at[dz], pr_sem.at[dz], zpeer(dz)) for dz in ORDER}
    q_copies = {
        dz: remote(qsend.at[dz], qbuf.at[NZ - dz], qs_sem.at[dz], qr_sem.at[NZ - dz], zpeer(dz)) for dz in ORDER}
    t_copies = {
        dz: remote(qsend.at[dz, 0:8], qbuf.at[NZ - dz, 0:8], qs_sem.at[dz], qr_sem.at[NZ - dz], zpeer(dz))
        for dz in ORDER}

    def answer(group, fn, rows):
        shares = [fn(lax.rem(z + dz, NZ), dz) for dz in group]
        for dz, value in zip(group, shares):
            qsend[dz, 0:rows] = value

    def collect_shares(total, copies, rows):
        for dz in ORDER:
            copies[dz].wait_recv()
        for dz in range(1, NZ):
            total = total + qbuf[dz, 0:rows]
        for dz in ORDER:
            copies[dz].wait_send()
        return total

    def exchange(fn, p, copies, rows):
        psend[...] = p
        for dz in FAR:
            p_copies[dz].start()
        total = fn(z, p)
        for group in GROUPS:
            for dz in group:
                p_copies[NZ - dz].wait_recv()
            answer(group, lambda i, dz: fn(i, pbuf[i]), rows)
            for dz in SENDS[group]:
                copies[dz].start()
        total = collect_shares(total, copies, rows)
        for dz in ORDER:
            p_copies[dz].wait_send()
        return total

    for group in ((4,), (3, 5), (2, 6), (1, 7)):
        answer(group, lambda i, dz: rhs_share(i), U)
        for dz in group:
            q_copies[dz].start()
    add_gram(False)
    scale = 2.0 / ITEMS
    g = (gacc[0:128, 0:128] + gacc[0:128, 128:256] + gacc[128:256, 0:128] + gacc[128:256, 128:256]) * scale
    gwide = jnp.concatenate(split2(g), axis=1)

    def turn(i, carry):
        for t in range(KH):
            cols = slice(t * 128, (t + 1) * 128)
            fn[i, cols, :] = ft[i, :, cols].astype(F32).T.astype(BF16)
        fn[i, SLOTS:SLOTS + 128, :] = gwide
        return carry

    lax.fori_loop(0, NZ, turn, 0)
    rhs = collect_shares(rhs_share(z), q_copies, U)

    def norm(v):
        return jnp.sum(v * v, axis=1, keepdims=True)

    def iterate(_, carry):
        sol, res, p, rr = carry
        q = p + exchange(share, p, q_copies, U)
        alpha = rr / jnp.sum(p * q, axis=1, keepdims=True)
        sol = sol + alpha * p
        res = res - alpha * q
        new = norm(res)
        return sol, res, res + (new / rr) * p, new

    carry = (jnp.zeros_like(rhs), rhs, rhs, norm(rhs))
    sol, res, p, rr = lax.fori_loop(0, ITERS - 1, iterate, carry)
    folded = exchange(last_share, p, t_copies, 8)
    block = lax.shift_right_logical(iota((8, 128), 1), 5)
    pq = norm(p) + jnp.concatenate(
        [jnp.sum(jnp.where(block == c, folded, 0.0), axis=1, keepdims=True) for c in range(4)], axis=0)
    sol = sol + (rr / pq) * p

    def group_rows(dy, c):
        return pl.ds(pl.multiple_of((lax.rem(y + dy, NY) * 2 + c) * U, U), U)

    gat[group_rows(0, core), :] = sol
    mine = gat.at[group_rows(0, core)]
    y_copies = [remote(mine, mine, ys_sem.at[dy], yr_sem.at[dy], ypeer(dy)) for dy in range(1, NY)]
    s_copies = [
        remote(gat.at[group_rows(dy, core)], gat.at[group_rows(dy, core)], ss_sem.at[dy], sr_sem.at[dy], sibling)
        for dy in range(NY)
    ]
    for copy in reversed(y_copies):
        copy.start()
    s_copies[0].start()
    for dy in (1, 7, 2, 6, 3, 5, 4):
        y_copies[NY - dy - 1].wait_recv()
        s_copies[dy].start()
    for copy in s_copies:
        copy.wait_recv()
    hml = jnp.concatenate(split3(gat[...]), axis=1)
    placed = jnp.dot(place[...], hml, preferred_element_type=F32)
    out_ref[...] = placed[:, 0:128] + placed[:, 128:256] + placed[:, 256:384]

    for copy in right + left + [fwd_right, fwd_left] + to_sib + ent_copies + y_copies + s_copies:
        copy.wait_send()


def per_device(item_table, neighbours, confidence, valid_counts, row_targets):
    dma = pltpu.SemaphoreType.DMA
    return pl.pallas_call(
        kernel,
        out_shape=jax.ShapeDtypeStruct((512, D), F32),
        in_specs=[pl.BlockSpec(memory_space=pltpu.HBM)] * 5,
        out_specs=pl.BlockSpec(memory_space=pltpu.VMEM),
        scratch_shapes=[
            pltpu.SMEM((U,), I32), pltpu.VMEM((U, K), I32), pltpu.VMEM((U, K), F32), pltpu.VMEM((1, 512), I32),
            pltpu.VMEM((TAB, D), F32), pltpu.VMEM((TAB, D), F32), pltpu.VMEM((TAB, D), F32), pltpu.VMEM((TAB, D), F32),
            pltpu.VMEM((U, K), I32), pltpu.VMEM((U, K), I32), pltpu.VMEM((4, U, K), F32),
            pltpu.VMEM((128, U * K), BF16), pltpu.VMEM((4 * 64, U * K), BF16),
            pltpu.VMEM((NZ, 24, 128), F32), pltpu.VMEM((NZ, 24, 128), F32), pltpu.VMEM((2, NZ, 24, 128), F32),
            pltpu.VMEM((2 * NX, SLOTS), F32), pltpu.VMEM((2 * D, TAB), BF16), pltpu.VMEM((4, 2 * D, 128), F32),
            pltpu.VMEM((NZ, 2 * D, SLOTS), BF16), pltpu.VMEM((NZ, SLOTS + 128, 2 * D), BF16),
            pltpu.VMEM((NZ, U, SLOTS), F32), pltpu.VMEM((NZ, U, SLOTS), F32), pltpu.VMEM((2 * D, 2 * D), F32),
            pltpu.VMEM((U, D), F32), pltpu.VMEM((NZ, U, D), F32),
            pltpu.VMEM((NZ, U, D), F32), pltpu.VMEM((NZ, U, D), F32),
            pltpu.VMEM((512, D), F32), pltpu.VMEM((512, 512), BF16),
            dma((4,)), dma, dma((4,)), dma((6,)), dma((2,)), dma((6,)), dma((6,)), dma((7,)), dma((7,)),
            dma((NZ,)), dma((NZ,)), dma((NZ,)), dma((NZ,)), dma((NY,)), dma((NY,)), dma((NY,)), dma((NY,)),
        ],
        compiler_params=pltpu.CompilerParams(
            collective_id=0, has_side_effects=True, vmem_limit_bytes=60 * 1024 * 1024),
    )(valid_counts, neighbours, confidence, row_targets.reshape(1, 512), item_table)


def solution(mesh):
    return jax.shard_map(
        per_device,
        mesh=mesh,
        in_specs=(
            P("shard", None),
            P(("replica", "shard"), None),
            P(("replica", "shard"), None),
            P(("replica", "shard")),
            P("shard"),
        ),
        out_specs=P("shard", None),
        check_vma=False,
    )
```

```python
import math

import jax
import jax.numpy as jnp
from jax import lax
from jax.experimental import pallas as pl
from jax.experimental.pallas import tpu as pltpu
from jax.sharding import PartitionSpec as P

ITERS = 4
NX, NZ, NY = 4, 8, 8
D = 128
K = 128
U = 32
TAB = 2048
ITEMS = 65536
CAP = 192
SLOTS = NX * CAP
KH = SLOTS // 128
MESH = pl.DeviceIdType.MESH
F32, BF16, I32 = jnp.float32, jnp.bfloat16, jnp.int32
ORDER = (1, 7, 2, 6, 3, 5, 4)
FAR = (4, 3, 5, 2, 6, 1, 7)
GROUPS = ((1, 7), (2, 6), (3, 5), (4,))
SENDS = {(1, 7): (), (2, 6): (), (3, 5): (), (4,): (4, 3, 5, 2, 6, 1, 7)}
NT = (((1,), (1,)), ((), ()))
TN = (((0,), (0,)), ((), ()))


def split2(v):
    hi = v.astype(BF16)
    lo = (v - hi.astype(F32)).astype(BF16)
    return hi, lo


def split3(v):
    hi = v.astype(BF16)
    rest = v - hi.astype(F32)
    mid = rest.astype(BF16)
    lo = (rest - mid.astype(F32)).astype(BF16)
    return hi, mid, lo


def iota(shape, dim):
    return lax.broadcasted_iota(I32, shape, dim)


def kernel(
    counts_hbm, ids_hbm, conf_hbm, targ_hbm, table,
    out_ref,
    counts, ids_ref, conf_ref, targ_ref,
    tab0, tab1, tab2, tab3, code_s, kl_s, val_s, a_s, b_s, ent_send, ent, ent2, idr, tt, halves, ft, fn, mw, mb, gacc,
    psend, pbuf, qsend, qbuf, gat, place,
    in_sem, own_sem, tx_sem, trx_sem, tfwd_sem, ts_sem, tsr_sem, es_sem, er_sem, ps_sem, pr_sem, qs_sem, qr_sem,
    ys_sem, yr_sem, ss_sem, sr_sem,
):
    r = lax.axis_index("replica")
    s = lax.axis_index("shard")
    z, x = lax.div(s, NX), lax.rem(s, NX)
    y, core = lax.div(r, 2), lax.rem(r, 2)

    def zpeer(dz):
        return (r, lax.rem(z + dz, NZ) * NX + x)

    def xpeer(dx):
        return (r, z * NX + lax.rem(x + dx, NX))

    def ypeer(dy):
        return (lax.rem(y + dy, NY) * 2 + core, s)

    sibling = (y * 2 + 1 - core, s)

    loads = [
        pltpu.make_async_copy(src, dst, in_sem.at[i])
        for i, (src, dst) in enumerate(
            [(ids_hbm, ids_ref), (counts_hbm, counts), (conf_hbm, conf_ref), (targ_hbm, targ_ref)])
    ]
    own = pltpu.make_async_copy(table, tab0, own_sem)
    for load in loads:
        load.start()
    own.start()

    barrier = pltpu.get_barrier_semaphore()
    peers = [zpeer(dz) for dz in range(1, NZ)] + [xpeer(1), xpeer(3), sibling]
    peers += [ypeer(dy) for dy in range(1, NY)]
    for peer in peers:
        pl.semaphore_signal(barrier, inc=1, device_id=peer, device_id_type=MESH)

    half = TAB // 2
    piece = half // 2

    def rows_of(c):
        return pl.ds(pl.multiple_of(core * half + c * piece, piece), piece)

    def remote(src, dst, send, recv, peer):
        return pltpu.make_async_remote_copy(
            src_ref=src, dst_ref=dst, send_sem=send, recv_sem=recv, device_id=peer, device_id_type=MESH)

    right = [remote(table.at[rows_of(c)], tab3.at[rows_of(c)], tx_sem.at[c], trx_sem.at[c], xpeer(1)) for c in range(2)]
    left = [remote(table.at[rows_of(c)], tab1.at[rows_of(c)], tx_sem.at[2 + c], trx_sem.at[2 + c], xpeer(3)) for c in range(2)]
    fwd_right = remote(tab3.at[rows_of(0)], tab2.at[rows_of(0)], tfwd_sem.at[0], trx_sem.at[4], xpeer(1))
    fwd_left = remote(tab1.at[rows_of(1)], tab2.at[rows_of(1)], tfwd_sem.at[1], trx_sem.at[5], xpeer(3))
    arrivals = [(tab3, 0), (tab1, 1), (tab3, 1), (tab1, 0), (tab2, 0), (tab2, 1)]
    to_sib = [
        remote(t.at[rows_of(c)], t.at[rows_of(c)], ts_sem.at[i], tsr_sem.at[i], sibling)
        for i, (t, c) in enumerate(arrivals)
    ]

    for load in loads[:3]:
        load.wait()
    ids = ids_ref[...]
    owner = lax.shift_right_logical(ids, 11)
    local = ids & (TAB - 1)
    rowi = iota((U, K), 0)
    lane = iota((U, K), 1)
    cnt = jnp.zeros((U, K), I32)
    for u in range(U):
        cnt = jnp.where(rowi == u, counts[u], cnt)
    used = lane < cnt
    key = jnp.where(used, owner, -1)
    e_all = jnp.concatenate(
        [jnp.where(key == o, 1.0, 0.0).astype(BF16) for o in range(NX * NZ)], axis=0)
    br, bc = iota((256, 256), 0), iota((256, 256), 1)
    lower = jnp.where((lax.shift_right_logical(br, 5) == lax.shift_right_logical(bc, 5)) & (bc < br), 1.0, 0.0).astype(BF16)
    x_all = jnp.concatenate(
        [jnp.dot(lower, e_all[i * 256:(i + 1) * 256], preferred_element_type=F32).astype(BF16) for i in range(4)], axis=0)
    tr, tc = iota((256, 128), 0), iota((256, 128), 1)
    tri = jnp.where((tr >= 128) | (tr < tc), 1.0, 0.0).astype(BF16)
    pos_all = jnp.dot(jnp.concatenate([e_all, x_all], axis=1), tri, preferred_element_type=F32)
    pos = jnp.zeros((U, K), F32)
    for o in range(NX * NZ):
        pos = jnp.where(key == o, pos_all[o * U:(o + 1) * U], pos)
    pos = pos.astype(I32)
    ox = owner & (NX - 1)
    full = pos < 128
    part = jnp.where(full, lax.shift_right_logical(pos, 6), ox & 1)
    row = jnp.where(full, ox, NX + lax.shift_right_logical(ox, 1))
    code_s[...] = jnp.where(used, part * 64 + lax.shift_right_logical(owner, 2) * 8 + row, -1)
    kl_s[...] = pos & 63
    m1, m2 = split2(conf_ref[...])
    val_s[0] = (local & 0xFF).astype(F32)
    val_s[1] = (rowi * 8 + lax.shift_right_logical(local, 8)).astype(F32)
    val_s[2] = m1.astype(F32)
    val_s[3] = m2.astype(F32)
    sub = iota((128, 128), 0)

    def build(u, carry):
        cols = pl.ds(pl.multiple_of(u * 128, 128), 128)
        a_s[:, cols] = jnp.where(sub == code_s[pl.ds(u, 1), :], 1.0, 0.0).astype(BF16)
        hot = sub[0:64] == kl_s[pl.ds(u, 1), :]
        for c in range(4):
            b_s[c * 64:(c + 1) * 64, cols] = jnp.where(hot, val_s[c, pl.ds(u, 1), :], 0.0).astype(BF16)
        return carry

    lax.fori_loop(0, U, build, 0)
    packed = lax.dot_general(b_s[...], a_s[...], NT, preferred_element_type=F32)

    def tiles(v):
        return jnp.concatenate([v[:, 0:64], v[:, 64:128]], axis=0).T.reshape(NZ, 8, 128)

    coded = packed[64:128].astype(I32)
    ent_send[:, 0:8, :] = tiles(packed[0:64] + ((coded & 7) * 256).astype(F32))
    ent_send[:, 8:16, :] = tiles(lax.shift_right_logical(coded, 3).astype(F32))
    ent_send[:, 16:24, :] = tiles(packed[128:192] + packed[192:256])
    ent[z] = ent_send[z]

    pl.semaphore_wait(barrier, len(peers))
    ent_copies = [
        remote(ent_send.at[lax.rem(z + dz, NZ)], ent.at[z], es_sem.at[i], er_sem.at[i], zpeer(dz))
        for i, dz in enumerate(ORDER)
    ]
    for copy in reversed(ent_copies):
        copy.start()
    right[0].start()
    left[1].start()
    right[1].start()
    left[0].start()

    loads[3].wait()
    place[...] = jnp.where(iota((512, 512), 0) == targ_ref[...], 1.0, 0.0).astype(BF16)

    def add_gram(first):
        g = lax.dot_general(tt[...], tt[...], NT, preferred_element_type=F32)
        gacc[...] = g if first else gacc[...] + g

    def transpose(tab, first, last=False):
        for c in range(TAB // 128):
            hi, lo = split2(tab[c * 128:(c + 1) * 128, :].T)
            tt[0:128, c * 128:(c + 1) * 128] = hi
            tt[128:256, c * 128:(c + 1) * 128] = lo
        if not last:
            add_gram(first)

    own.wait()
    transpose(tab0, True)

    for copy in ent_copies:
        copy.wait_recv()

    xr = [lax.rem(x + rel, NX) for rel in range(NX)]
    for i in range(NZ):
        ent2[0, i] = ent[i]
        ent2[1, i] = pltpu.roll(ent[i], 64, 1)
    low = iota((1, 128), 1) < 64

    def full_row(i, c, rel):
        return ent[i, pl.ds(c * 8 + xr[rel], 1), :]

    def half_row(i, c, rel, d):
        return ent2[lax.rem(xr[rel] + d, 2), i, pl.ds(c * 8 + NX + lax.div(xr[rel], 2), 1), :]

    for rel in range(NX):
        for g in range(2):
            row = rel * 2 + g
            for t in range(4):
                idr[row:row + 1, t * 128:(t + 1) * 128] = full_row(4 * g + t, 0, rel)
            for t in range(2):
                a = 4 * g + 2 * t
                first, second = (a, a + 1) if rel % 2 == 0 else (a + 1, a)
                idr[row:row + 1, 512 + t * 128:640 + t * 128] = jnp.where(
                    low, half_row(first, 0, rel, 0), half_row(second, 0, rel, 1))

    ucode = iota((U, 128), 0).astype(F32)
    for i in range(NZ):
        for t in range(KH):
            if t < NX:
                user, m = full_row(i, 1, t), full_row(i, 2, t)
            else:
                pair = 2 * (t - NX)
                first, second = (pair, pair + 1) if i % 2 == 0 else (pair + 1, pair)
                user = jnp.where(low, half_row(i, 1, first, 0), half_row(i, 1, second, 1))
                m = jnp.where(low, half_row(i, 2, first, 0), half_row(i, 2, second, 1))
            eq = user == ucode
            mw[i, :, t * 128:(t + 1) * 128] = jnp.where(eq, m * (1.0 / D), 0.0)
            mb[i, :, t * 128:(t + 1) * 128] = jnp.where(eq & (m > 0.0), (1.0 + m) * (1.0 / math.sqrt(D)), 0.0)

    def collect(rel, other):
        def group(g, carry):
            wanted = idr[pl.ds(rel * 2 + g, 1), :]
            item = iota((256, SLOTS), 0).astype(F32)
            acc = None
            for b in range(TAB // 256):
                hot = jnp.where(item == wanted - b * 256.0, 1.0, 0.0).astype(BF16)
                d = jnp.dot(tt[:, b * 256:(b + 1) * 256], hot, preferred_element_type=F32)
                acc = d if acc is None else acc + d
            for t in range(4):
                ft[4 * g + t, :, rel * 128:(rel + 1) * 128] = acc[:, t * 128:(t + 1) * 128].astype(BF16)
            for t in range(2):
                now = acc[:, 512 + t * 128:640 + t * 128]
                if other is None:
                    halves[2 * g + t] = now
                else:
                    then = halves[2 * g + t]
                    even, odd = (now, then) if rel % 2 == 0 else (then, now)
                    keep = iota((256, 128), 1) < 64
                    cols = slice((NX + rel // 2) * 128, (NX + rel // 2 + 1) * 128)
                    ft[4 * g + 2 * t, :, cols] = jnp.where(keep, even, odd).astype(BF16)
                    ft[4 * g + 2 * t + 1, :, cols] = jnp.where(keep, odd, even).astype(BF16)
            return carry

        lax.fori_loop(0, 2, group, 0)

    right[0].wait_recv()
    fwd_right.start()
    to_sib[0].start()
    left[1].wait_recv()
    fwd_left.start()
    to_sib[1].start()
    collect(0, None)
    left[0].wait_recv()
    to_sib[3].start()
    right[1].wait_recv()
    to_sib[2].start()
    for i in (1, 3):
        to_sib[i].wait_recv()
    transpose(tab1, False)
    collect(1, 0)
    for i in (0, 2):
        to_sib[i].wait_recv()
    transpose(tab3, False)
    fwd_right.wait_recv()
    to_sib[4].start()
    fwd_left.wait_recv()
    to_sib[5].start()
    collect(3, None)
    for i in (4, 5):
        to_sib[i].wait_recv()
    transpose(tab2, False, True)
    collect(2, 3)

    def fold(res):
        return res[0:U, 0:128] + res[0:U, 128:256] + res[U:2 * U, 0:128]

    def rhs_share(i):
        hi, lo = split2(mb[i])
        return fold(lax.dot_general(
            jnp.concatenate([hi, lo], axis=0), ft[i], NT, preferred_element_type=F32))

    def project(i, hi, lo):
        lhs = jnp.concatenate(
            [jnp.concatenate([hi, hi], axis=1), jnp.concatenate([lo, jnp.zeros_like(lo)], axis=1)], axis=0)
        res = jnp.dot(lhs, ft[i], preferred_element_type=F32)
        return res[0:U] + res[U:2 * U]

    def share(blocks, vectors):
        parts = [split2(p) for p in vectors]
        grams = jnp.dot(
            jnp.concatenate([v for pair in parts for v in pair], axis=0), fn[0, SLOTS:SLOTS + 128, :],
            preferred_element_type=F32)
        out = []
        for k, (i, (hi, lo)) in enumerate(zip(blocks, parts)):
            both = jnp.concatenate(split2(mw[i] * project(i, hi, lo)), axis=0)
            res = jnp.dot(both, fn[i, 0:SLOTS, :], preferred_element_type=F32)
            out.append(fold(res + grams[2 * U * k:2 * U * (k + 1)]))
        return out

    def last_shares(blocks, vectors):
        return [last_share(i, p) for i, p in zip(blocks, vectors)]

    def last_share(i, p):
        hi, lo = split2(p)
        proj = project(i, hi, lo)
        sq = mw[i] * proj * proj
        t = fold(jnp.dot(
            jnp.concatenate([hi, lo], axis=0), fn[i, SLOTS:SLOTS + 128, :], preferred_element_type=F32)) * p
        for kh in range(KH):
            t = t + sq[:, kh * 128:(kh + 1) * 128]
        block = lax.shift_right_logical(iota((8, 128), 1), 5)
        folded = jnp.zeros((8, 128), F32)
        for c in range(4):
            v = t[c * 8:(c + 1) * 8]
            v = v + pltpu.roll(v, 64, 1)
            v = v + pltpu.roll(v, 32, 1)
            folded = jnp.where(block == c, v, folded)
        return folded

    p_copies = {dz: remote(psend, pbuf.at[z], ps_sem.at[dz], pr_sem.at[dz], zpeer(dz)) for dz in ORDER}
    q_copies = {
        dz: remote(qsend.at[dz], qbuf.at[NZ - dz], qs_sem.at[dz], qr_sem.at[NZ - dz], zpeer(dz)) for dz in ORDER}
    t_copies = {
        dz: remote(qsend.at[dz, 0:8], qbuf.at[NZ - dz, 0:8], qs_sem.at[dz], qr_sem.at[NZ - dz], zpeer(dz))
        for dz in ORDER}

    def answer(group, fn, rows):
        for dz, value in zip(group, fn([lax.rem(z + dz, NZ) for dz in group])):
            qsend[dz, 0:rows] = value

    def collect_shares(total, copies, rows):
        for dz in ORDER:
            copies[dz].wait_recv()
        for dz in range(1, NZ):
            total = total + qbuf[dz, 0:rows]
        for dz in ORDER:
            copies[dz].wait_send()
        return total

    def exchange(fn, p, copies, rows):
        psend[...] = p
        for dz in FAR:
            p_copies[dz].start()
        total = fn([z], [p])[0]
        for group in GROUPS:
            for dz in group:
                p_copies[NZ - dz].wait_recv()
            answer(group, lambda blocks: fn(blocks, [pbuf[i] for i in blocks]), rows)
            for dz in SENDS[group]:
                copies[dz].start()
        total = collect_shares(total, copies, rows)
        for dz in ORDER:
            p_copies[dz].wait_send()
        return total

    for group in ((4,), (3, 5), (2, 6), (1, 7)):
        answer(group, lambda blocks: [rhs_share(i) for i in blocks], U)
        for dz in group:
            q_copies[dz].start()
    add_gram(False)
    scale = 2.0 / ITEMS
    g = (gacc[0:128, 0:128] + gacc[0:128, 128:256] + gacc[128:256, 0:128] + gacc[128:256, 128:256]) * scale
    gwide = jnp.concatenate(split2(g), axis=1)

    def turn(i, carry):
        for t in range(KH):
            cols = slice(t * 128, (t + 1) * 128)
            fn[i, cols, :] = ft[i, :, cols].astype(F32).T.astype(BF16)
        fn[i, SLOTS:SLOTS + 128, :] = gwide
        return carry

    lax.fori_loop(0, NZ, turn, 0)
    rhs = collect_shares(rhs_share(z), q_copies, U)

    def norm(v):
        return jnp.sum(v * v, axis=1, keepdims=True)

    def iterate(_, carry):
        sol, res, p, rr = carry
        q = p + exchange(share, p, q_copies, U)
        alpha = rr / jnp.sum(p * q, axis=1, keepdims=True)
        sol = sol + alpha * p
        res = res - alpha * q
        new = norm(res)
        return sol, res, res + (new / rr) * p, new

    carry = (jnp.zeros_like(rhs), rhs, rhs, norm(rhs))
    sol, res, p, rr = lax.fori_loop(0, ITERS - 1, iterate, carry)
    folded = exchange(last_shares, p, t_copies, 8)
    block = lax.shift_right_logical(iota((8, 128), 1), 5)
    pq = norm(p) + jnp.concatenate(
        [jnp.sum(jnp.where(block == c, folded, 0.0), axis=1, keepdims=True) for c in range(4)], axis=0)
    sol = sol + (rr / pq) * p

    def group_rows(dy, c):
        return pl.ds(pl.multiple_of((lax.rem(y + dy, NY) * 2 + c) * U, U), U)

    gat[group_rows(0, core), :] = sol
    mine = gat.at[group_rows(0, core)]
    y_copies = [remote(mine, mine, ys_sem.at[dy], yr_sem.at[dy], ypeer(dy)) for dy in range(1, NY)]
    s_copies = [
        remote(gat.at[group_rows(dy, core)], gat.at[group_rows(dy, core)], ss_sem.at[dy], sr_sem.at[dy], sibling)
        for dy in range(NY)
    ]
    for copy in reversed(y_copies):
        copy.start()
    s_copies[0].start()
    for dy in (1, 7, 2, 6, 3, 5, 4):
        y_copies[NY - dy - 1].wait_recv()
        s_copies[dy].start()
    for copy in s_copies:
        copy.wait_recv()
    hml = jnp.concatenate(split3(gat[...]), axis=1)
    placed = jnp.dot(place[...], hml, preferred_element_type=F32)
    out_ref[...] = placed[:, 0:128] + placed[:, 128:256] + placed[:, 256:384]

    for copy in right + left + [fwd_right, fwd_left] + to_sib + ent_copies + y_copies + s_copies:
        copy.wait_send()


def per_device(item_table, neighbours, confidence, valid_counts, row_targets):
    dma = pltpu.SemaphoreType.DMA
    return pl.pallas_call(
        kernel,
        out_shape=jax.ShapeDtypeStruct((512, D), F32),
        in_specs=[pl.BlockSpec(memory_space=pltpu.HBM)] * 5,
        out_specs=pl.BlockSpec(memory_space=pltpu.VMEM),
        scratch_shapes=[
            pltpu.SMEM((U,), I32), pltpu.VMEM((U, K), I32), pltpu.VMEM((U, K), F32), pltpu.VMEM((1, 512), I32),
            pltpu.VMEM((TAB, D), F32), pltpu.VMEM((TAB, D), F32), pltpu.VMEM((TAB, D), F32), pltpu.VMEM((TAB, D), F32),
            pltpu.VMEM((U, K), I32), pltpu.VMEM((U, K), I32), pltpu.VMEM((4, U, K), F32),
            pltpu.VMEM((128, U * K), BF16), pltpu.VMEM((4 * 64, U * K), BF16),
            pltpu.VMEM((NZ, 24, 128), F32), pltpu.VMEM((NZ, 24, 128), F32), pltpu.VMEM((2, NZ, 24, 128), F32),
            pltpu.VMEM((2 * NX, SLOTS), F32), pltpu.VMEM((2 * D, TAB), BF16), pltpu.VMEM((4, 2 * D, 128), F32),
            pltpu.VMEM((NZ, 2 * D, SLOTS), BF16), pltpu.VMEM((NZ, SLOTS + 128, 2 * D), BF16),
            pltpu.VMEM((NZ, U, SLOTS), F32), pltpu.VMEM((NZ, U, SLOTS), F32), pltpu.VMEM((2 * D, 2 * D), F32),
            pltpu.VMEM((U, D), F32), pltpu.VMEM((NZ, U, D), F32),
            pltpu.VMEM((NZ, U, D), F32), pltpu.VMEM((NZ, U, D), F32),
            pltpu.VMEM((512, D), F32), pltpu.VMEM((512, 512), BF16),
            dma((4,)), dma, dma((4,)), dma((6,)), dma((2,)), dma((6,)), dma((6,)), dma((7,)), dma((7,)),
            dma((NZ,)), dma((NZ,)), dma((NZ,)), dma((NZ,)), dma((NY,)), dma((NY,)), dma((NY,)), dma((NY,)),
        ],
        compiler_params=pltpu.CompilerParams(
            collective_id=0, has_side_effects=True, vmem_limit_bytes=60 * 1024 * 1024),
    )(valid_counts, neighbours, confidence, row_targets.reshape(1, 512), item_table)


def solution(mesh):
    return jax.shard_map(
        per_device,
        mesh=mesh,
        in_specs=(
            P("shard", None),
            P(("replica", "shard"), None),
            P(("replica", "shard"), None),
            P(("replica", "shard")),
            P("shard"),
        ),
        out_specs=P("shard", None),
        check_vma=False,
    )
```
